128 devices in a mesh: attn: 8 (over y, core), tp: 4 (over z), exp: 4 (over x).
Axes of the slice: x: 4, y: 4, z: 4, core: 2. Of those that a mesh axis runs over, the one named last changes fastest.
Arguments:
- new_query: bfloat16 [768, 3072], P(('attn', 'exp'), 'tp'), may hold values from -120 to 120
- new_kv: bfloat16 [768, 2, 512], P(('attn', 'exp'), None, 'tp'), may hold values from -4.5 to 4.5
- kv_cache: bfloat16 [768, 2, 512, 512], P(('attn', 'exp'), None, None, 'tp'), may hold values from -4.5 to 4.5
- lengths: int32 [768], P(('attn', 'exp')), may hold values from 2 to 512
- residual: bfloat16 [768, 6144], P(('attn', 'exp')), may hold values from -25 to 25
- out_proj: bfloat16 [3072, 6144], P('tp'), may hold values from -0.109375 to 0.109375
- expert_ids: int32 [768, 2], P(('attn', 'exp')), may hold values from 0 to 3, all different within a row; in each aligned block of 24 rows (0 to 23, 24 to 47, ...) at most 18 rows name the same one
- gate_weights: float32 [768, 2], P(('attn', 'exp')), may hold values from 0.1 to 1
- slot_expert: int32 [4], replicated, may hold values from 0 to 3, as said below
- moe_gain: float32 [6144], replicated, may hold values from 0.25 to 1.75
- w_gate: bfloat16 [4, 6144, 8192], P('exp', None, ('attn', 'tp')), may hold values from -0.078125 to 0.078125
- w_up: bfloat16 [4, 6144, 8192], P('exp', None, ('attn', 'tp')), may hold values from -0.078125 to 0.078125
- w_down: bfloat16 [4, 8192, 6144], P('exp', ('attn', 'tp')), may hold values from -0.125 to 0.125
Outputs:
- layer_out: bfloat16 [768, 6144], P(('attn', 'exp'), 'tp')
The draws below stay inside these ranges and needn't reach their ends.
Inputs may be any that keep to these rules, and one draw needn't show every extreme that they name: `expert_ids`: in the rows of one device (aligned blocks of 24 requests) no expert is named more than 18 times, and that number is reached; a token's two experts differ. `slot_expert`: each expert is loaded in exactly one slot.
All inputs are finite; a program needn't handle non-finite values.
Results may differ from the reference program's by a relative error of at most 0.0059.
Values may be sent and summed in bfloat16 or wider, within the bound.
A program may use at most 128 MiB of HBM per device.

```python
import math
import jax
import jax.numpy as jnp
import numpy as np
from jax import lax

D = 6144
HQ = 24
HK = 4
HD = 128
EXPERTS = 4
FF_WIN = 8192
CACHE = 512
R_DEV = 24
CAP = 18
REQ = 768


def entries(key):
    first_key = jnp.clip(jax.random.normal(jax.random.fold_in(key, 71), (REQ, HK * HD), jnp.float32), -4.5, 4.5)
    return first_key


def draw_kv_cache(key, part):
    first_key = entries(key)
    key = jax.random.fold_in(key, 3)
    drawn_cache = jnp.clip(jax.random.normal(key, (REQ, 2, CACHE, HK * HD), jnp.float32), -4.5, 4.5)
    drawn_cache = drawn_cache.at[:, 0, 0, :].set(first_key)
    return drawn_cache.astype(jnp.bfloat16)


def draw_new_query(key, part):
    key = jax.random.fold_in(key, 5)
    drawn_query = jnp.clip(jax.random.normal(key, (REQ, HQ * HD), jnp.float32), -4.5, 4.5)
    return drawn_query.astype(jnp.bfloat16)


def draw_lengths(key, part):
    key = jax.random.fold_in(key, 7)
    drawn = jax.random.randint(key, (REQ,), 2, CACHE + 1)
    return drawn.at[0].set(CACHE).astype(jnp.int32)


def draw_slot_expert(key, part):
    key = jax.random.fold_in(key, 11)
    return jax.random.permutation(key, EXPERTS).astype(jnp.int32)


def draw_residual(key, part):
    key = jax.random.fold_in(key, 9)
    key_base, key_rows, key_cols = jax.random.split(key, 3)
    base_rows = jnp.clip(jax.random.normal(key_base, (REQ, D), jnp.float32), -4.0, 4.0)
    row_scale = jnp.exp(jax.random.uniform(key_rows, (REQ, 1), jnp.float32, jnp.log(0.3), jnp.log(3.0)))
    col_scale = jnp.exp(jax.random.uniform(key_cols, (1, D), jnp.float32, jnp.log(0.5), jnp.log(2.0)))
    return (base_rows * row_scale * col_scale).astype(jnp.bfloat16)


def spiked(values, key, source, target, shards_of, factor):
    owner, partner = [(jnp.arange(values.shape[position]) // (values.shape[position] // shards_of)).reshape([-1 if axis == position else 1 for axis in range(values.ndim)]) for position in (source, target)]
    chosen = jax.random.permutation(key, shards_of)[partner]
    strong = (owner == chosen) | (owner == (partner + shards_of // 2) % shards_of)
    return jnp.where(strong, factor * values, values)


def block_scale(key, extent, pieces, low, largest):
    def one(position, parts):
        steps = jax.random.uniform(jax.random.fold_in(jax.random.fold_in(key, 6), position), (parts,), jnp.float32, low / len(pieces), largest / len(pieces))
        return jnp.repeat(jnp.exp(steps), extent[position] // parts).reshape((-1,) + (1,) * (len(extent) - position - 1))

    level = one(*pieces[0])
    for cut in pieces[1:]:
        level = level * one(*cut)
    return level


def deal_out(own_key, own, number, rows, amount, top, reach, skew):
    ranking = jax.random.permutation(own_key, amount)
    heavy_load, ordinary = shares(amount, rows * top, reach, skew, True), shares(amount, rows * top, reach, skew, False)
    places = jnp.arange(amount)

    def named(tallies, turn):
        used = int((tallies > 0).sum())
        fixed = max(1, used // 4)
        passed = fixed + (places - fixed + turn * (used - fixed)) % max(1, amount - fixed)
        return jnp.zeros((amount,), jnp.int32).at[ranking[jnp.where(places < fixed, places, passed)]].set(jnp.asarray(tallies, jnp.int32))

    tallies = jnp.where(number % 4 == 0, named(heavy_load, number // 4), named(ordinary, number - number // 4 - 1))
    mixed = jax.random.permutation(jax.random.fold_in(own, 3), amount)
    donor, taker = mixed[0:amount // 2 * 2:2], mixed[1:amount // 2 * 2:2]
    slack = jnp.minimum(tallies[donor] - 1, reach - tallies[taker]) // 2
    slack = jnp.where((donor == ranking[0]) | (taker == ranking[0]) | (tallies[taker] == 0), 0, jnp.maximum(slack, 0))
    passed = jax.random.randint(jax.random.fold_in(own, 4), (amount // 2,), 0, 1 << 20) % (slack + 1)
    tallies = tallies.at[donor].add(-passed).at[taker].add(passed)
    members = jnp.searchsorted(jnp.cumsum(tallies), jnp.arange(rows * top), side="right").astype(jnp.int32)
    listing = members.reshape(top, rows).T
    listing = listing[jax.random.permutation(jax.random.fold_in(own, 1), rows)]
    turn = jax.random.randint(jax.random.fold_in(own, 2), (rows, 1), 0, top)
    return jnp.take_along_axis(listing, (jnp.arange(top)[None, :] + turn) % top, axis=1)


def shares(count, total, most, skew, full):
    portions = [(1 << 20) // math.isqrt(standing ** skew) + 1 for standing in range(1, count + 1)]
    largest = most if full else min(most, max(-(-total // count), total * portions[0] // sum(portions)))
    least = 1 if total - largest >= count - 1 else 0
    given, surplus = [largest] + [least] * (count - 1), total - largest - least * (count - 1)
    while surplus > 0:
        candidates = [i for i in range(1, count) if given[i] < largest] or [i for i in range(1, count) if given[i] < most]
        pool, remaining = sum([portions[i] for i in candidates]), surplus
        for i in candidates:
            more = min(most - given[i], max(1, remaining * portions[i] // pool), surplus)
            given[i] = given[i] + more
            surplus = surplus - more
    return np.array(given)


def gaussian(key, dims, scale, bound, cuts=(), kind=jnp.bfloat16):
    gain = block_scale(key, dims, cuts, -0.22, 0.18) if cuts else 1.0
    entries = jax.random.normal(key, dims, jnp.float32) * scale * gain
    return jnp.minimum(jnp.maximum(entries, -bound), bound).astype(kind)


def noise_with(own_key, shape, deviation, limit, pieces, heavy, kind=jnp.bfloat16):
    entries = deviation * jax.random.normal(own_key, shape, jnp.float32)
    if pieces:
        entries = entries * block_scale(own_key, shape, pieces, -0.22, 0.18)
    return jnp.clip(spiked(entries, jax.random.fold_in(own_key, 3), *heavy), -limit, limit).astype(kind)


def setup_inputs(seed: int = 0) -> dict:
    splits = jax.random.split(jax.random.key(seed), 14)
    new_query = draw_new_query(jax.random.fold_in(splits[13], 71), 0)
    new_kv = gaussian(splits[1], (REQ, 2, HK * HD), 1.0, 4.5, ((0, 32), (2, 4)))
    kv_cache = draw_kv_cache(jax.random.fold_in(splits[13], 71), 0)
    lengths = draw_lengths(jax.random.fold_in(splits[13], 71), 0)
    residual = draw_residual(jax.random.fold_in(splits[13], 71), 0)
    out_proj = gaussian(splits[5], (HQ * HD, D), (HQ * HD) ** -0.5, 0.109375, ((0, 4),))
    expert_ids_keys = jax.random.split(jax.random.fold_in(splits[6], 1), REQ // R_DEV)
    expert_ids_turns = jax.random.permutation(jax.random.fold_in(splits[6], 3), REQ // R_DEV)
    expert_ids = jax.vmap(lambda own, number: deal_out(jax.random.fold_in(splits[6], 2), own, number, R_DEV, EXPERTS, 2, CAP, 1))(expert_ids_keys, expert_ids_turns).reshape((REQ, 2))
    gate_weights = jnp.clip(0.1 + 0.9 * jax.random.uniform(splits[7], (REQ, 2), jnp.float32) ** block_scale(splits[7], (REQ, 2), ((0, 32),), -0.2, 0.2), 0.1, 1.0)
    slot_expert = draw_slot_expert(jax.random.fold_in(splits[13], 71), 0)
    moe_gain = jnp.clip(1.0 + 0.15 * jax.random.normal(splits[9], (D,), jnp.float32), 0.25, 1.75)
    w_gate = gaussian(splits[10], (EXPERTS, D, FF_WIN), D ** -0.5, 0.078125, ((0, 4), (2, 32)))
    w_up = gaussian(splits[11], (EXPERTS, D, FF_WIN), D ** -0.5, 0.078125, ((0, 4), (2, 32)))
    w_down = noise_with(splits[12], (EXPERTS, FF_WIN, D), FF_WIN ** -0.5, 0.125, ((0, 4), (1, 32)), (1, 2, 32, 2.75))
    return dict(new_query=new_query, new_kv=new_kv, kv_cache=kv_cache, lengths=lengths, residual=residual, out_proj=out_proj, expert_ids=expert_ids, gate_weights=gate_weights, slot_expert=slot_expert, moe_gain=moe_gain, w_gate=w_gate, w_up=w_up, w_down=w_down)


def attend_one(pack):
    query_row, fresh, cached, used = pack
    per_group = HQ // HK
    score_scale = HD ** (-0.5)
    queries = query_row.astype(jnp.float32).reshape(HK, per_group, HD)
    key_rows = cached[0].astype(jnp.float32).reshape(CACHE, HK, HD)
    value_rows = cached[1].astype(jnp.float32).reshape(CACHE, HK, HD)
    fresh_key = fresh[0].astype(jnp.float32).reshape(HK, HD)
    fresh_value = fresh[1].astype(jnp.float32).reshape(HK, HD)
    scores = jnp.einsum('kgd,ckd->kgc', queries, key_rows) * score_scale
    own_score = jnp.einsum('kgd,kd->kg', queries, fresh_key) * score_scale
    visible = jnp.arange(CACHE, dtype=jnp.int32)[None, None, :] < used
    scores = jnp.where(visible, scores, -1e+30)
    highest = jnp.maximum(lax.optimization_barrier(jnp.max(scores, axis=2)), own_score)
    weights = jnp.exp(scores - highest[:, :, None])
    own_weight = jnp.exp(own_score - highest)
    denominator = lax.optimization_barrier(jnp.sum(weights, axis=2)) + own_weight
    probability = (weights / denominator[:, :, None]).astype(jnp.bfloat16).astype(jnp.float32)
    own_prob = (own_weight / denominator).astype(jnp.bfloat16).astype(jnp.float32)
    attended_sum = jnp.einsum('kgc,ckd->kgd', probability, value_rows) + own_prob[:, :, None] * fresh_value[:, None, :]
    return attended_sum.reshape(HQ * HD).astype(jnp.bfloat16)

def reference(new_query, new_kv, kv_cache, lengths, residual, out_proj, expert_ids, gate_weights, slot_expert, moe_gain, w_gate, w_up, w_down):
    attended = lax.map(attend_one, (new_query, new_kv, kv_cache, lengths))
    hidden = residual.astype(jnp.float32) + jnp.dot(attended, out_proj, preferred_element_type=jnp.float32)
    sent_rows = hidden.astype(jnp.bfloat16).astype(jnp.float32)
    spread = lax.optimization_barrier(jnp.mean(sent_rows * sent_rows, axis=1, keepdims=True))
    normed = (sent_rows * lax.rsqrt(spread + 1e-05) * moe_gain[None, :]).astype(jnp.bfloat16)

    def run_slot(slot_index):
        gate_part = jnp.dot(normed, w_gate[slot_index], preferred_element_type=jnp.float32)
        up_part = jnp.dot(normed, w_up[slot_index], preferred_element_type=jnp.float32)
        active = (jax.nn.silu(gate_part) * up_part).astype(jnp.bfloat16)
        return jnp.dot(active, w_down[slot_index], preferred_element_type=jnp.float32).astype(jnp.bfloat16)
    expert_out = lax.map(run_slot, jnp.arange(EXPERTS, dtype=jnp.int32))
    chosen = expert_ids[:, :, None] == slot_expert[None, None, :]
    slot_weight = lax.optimization_barrier(jnp.sum(jnp.where(chosen, gate_weights[:, :, None], 0.0), axis=1))
    expert_mix = jnp.einsum('rs,srd->rd', slot_weight, expert_out.astype(jnp.float32), precision=lax.Precision.HIGHEST)
    return (hidden + expert_mix).astype(jnp.bfloat16)
```

```python
import jax
import jax.numpy as jnp
from jax import lax
from jax.experimental import pallas as pl
from jax.experimental.pallas import tpu as pltpu
from jax.sharding import PartitionSpec as P

MESH = pl.DeviceIdType.MESH
F32 = jnp.float32
BF16 = jnp.bfloat16

HD = 128
HEADS = 6
R = 24
R2 = 48
CACHE = 512
D = 6144
QD = 1536
W = 256
SEMS = 288

STREAMS = (("x", "y", "z"), ("y", "z", "x"), ("z", "x", "y"))
FORWARD_UP = (0, 3)
FORWARD_DOWN = (1, 2)


def wrap(v):
    return lax.rem(v + 4, 4)


def kernel(
    lengths, slot_expert, query, new_kv, residual, ids, gate_w, gain, cache, out_proj, w_gate, w_up, w_down,
    out,
    k_buf, v_buf, op_buf, wg, wu, wd, q_pad, kn, vn, scores, attn_out,
    info, res_send, res_recv, z_send, z_recv, hidden,
    x_all, ssum, acc_g, acc_u, act,
    sib_out, sib_in, part, d2_in, plane_in, row_out, row_in, row_own, blk_out, blk_in, fin_send, fin,
    send_sems, recv_sems, local_sems,
):
    attn = lax.axis_index("attn")
    me = {"y": attn // 2, "c": lax.rem(attn, 2), "z": lax.axis_index("tp"), "x": lax.axis_index("exp")}
    c, other = me["c"], 1 - me["c"]

    def device(c=None, **steps):
        at = dict(me)
        for axis, step in steps.items():
            at[axis] = wrap(at[axis] + step)
        if c is not None:
            at["c"] = c
        return (at["y"] * 2 + at["c"], at["z"], at["x"])

    sibling = device(c=other)

    def local(src, dst, i):
        return pltpu.make_async_copy(src, dst, local_sems.at[i])

    k_copies = [local(cache.at[pl.ds(i * 6, 6), 0], k_buf.at[pl.ds(i * 6, 6)], i) for i in range(4)]
    v_copies = [local(cache.at[pl.ds(i * 6, 6), 1], v_buf.at[pl.ds(i * 6, 6)], 4 + i) for i in range(4)]
    op_copies = {
        j: local(out_proj.at[:, pl.ds(pl.multiple_of(wrap(me["z"] + j) * QD, QD), QD)], op_buf.at[j], 8 + j)
        for j in (2, 1, 3, 0)
    }
    w_copies = [local(w_gate.at[0], wg, 12), local(w_up.at[0], wu, 13)]
    wd_copies = []
    for half, h in ((0, c), (1, other)):
        for z in range(4):
            for s in range(3):
                start = pl.multiple_of(z * QD + s * 512 + h * W, W)
                wd_copies.append(
                    local(w_down.at[0, :, pl.ds(start, W)], wd.at[half, z, s], 14 + half * 12 + z * 3 + s)
                )
    for cp in k_copies + v_copies:
        cp.start()
    for j in (2, 1, 3, 0):
        op_copies[j].start()

    barrier = pltpu.get_barrier_semaphore()
    partners = [device(c=k, z=j) for j in (1, 2, 3) for k in (0, 1)] + [sibling]
    partners += [device(**{a: j}) for a in ("x", "y") for j in (1, 2, 3)]
    for p in partners:
        pl.semaphore_signal(barrier, inc=1, device_id=p, device_id_type=MESH)

    table = {}
    started = []

    def sem(key):
        if key not in table:
            table[key] = len(table)
            assert len(table) <= SEMS
        return table[key]

    def send(src, dst, key, to, index=None):
        i = sem(key)
        cp = pltpu.make_async_remote_copy(
            src_ref=src, dst_ref=dst, send_sem=send_sems.at[i],
            recv_sem=recv_sems.at[i if index is None else index],
            device_id=to, device_id_type=MESH,
        )
        cp.start()
        started.append(cp)

    def arrived(dst, key, index=None):
        i = sem(key) if index is None else index
        pltpu.make_async_remote_copy(
            src_ref=dst, dst_ref=dst, send_sem=send_sems.at[i], recv_sem=recv_sems.at[i],
            device_id=sibling, device_id_type=MESH,
        ).wait_recv()

    def drain():
        for cp in started:
            cp.wait_send()
        started.clear()

    z_sem = {}
    for j in range(4):
        z_sem[j] = sem(("zr", j, 0))
        sem(("zr", j, 1))

    lane = lax.broadcasted_iota(jnp.int32, (R, 128), 1)
    mine = jnp.zeros((R, 128), F32)
    for s in range(4):
        hit = jnp.where(ids[...] == slot_expert[s], gate_w[...], 0.0)
        mine = mine + jnp.where(lane == s, jnp.sum(hit, axis=1, keepdims=True), 0.0)
    info[c, me["y"], me["x"]] = mine

    def res_part(h):
        return jnp.concatenate(
            [residual[:, pl.ds(pl.multiple_of(me["z"] * QD + s * 512 + h * W, W), W)] for s in range(3)], axis=1
        ).astype(F32)

    res_send[...] = res_part(other)

    pl.semaphore_wait(barrier, len(partners))
    for j in (1, 3, 2):
        spot = info.at[c, me["y"], me["x"]]
        send(spot, spot, ("info x", j), device(x=j))
    send(res_send, res_recv, ("res",), sibling)

    for h in range(8):
        if h < HEADS:
            q_pad[pl.ds(h, R, stride=8), :] = query[:, h * HD : (h + 1) * HD].astype(F32)
        else:
            q_pad[pl.ds(h, R, stride=8), :] = jnp.zeros((R, HD), F32)
        kn[pl.ds(h, R, stride=8), :] = new_kv[:, :HD].astype(F32)
        vn[pl.ds(h, R, stride=8), :] = new_kv[:, HD:].astype(F32)
    scale = HD ** (-0.5)
    position = lax.broadcasted_iota(jnp.int32, (8, CACHE), 1)

    for i in range(4):
        k_copies[i].wait()
        for r in range(i * 6, i * 6 + 6):
            s = lax.dot_general(
                q_pad[r * 8 : r * 8 + 8, :].astype(BF16), k_buf[r], (((1,), (1,)), ((), ())),
                preferred_element_type=F32,
            ) * scale
            scores[r * 8 : r * 8 + 8, :] = jnp.where(position < lengths[r], s, -1e30)
    own_score = jnp.sum(q_pad[...] * kn[...], axis=1, keepdims=True) * scale
    raw = scores[...]
    top = jnp.maximum(jnp.max(raw, axis=1, keepdims=True), own_score)
    weight = jnp.exp(raw - top)
    own_weight = jnp.exp(own_score - top)
    total = jnp.sum(weight, axis=1, keepdims=True) + own_weight
    scores[...] = weight / total
    own_prob = (own_weight / total).astype(BF16).astype(F32)
    for i in range(4):
        v_copies[i].wait()
        for r in range(i * 6, i * 6 + 6):
            attn_out[r * 8 : r * 8 + 8, :] = jnp.dot(
                scores[r * 8 : r * 8 + 8, :].astype(BF16), v_buf[r], preferred_element_type=F32
            )
    attn_out[...] = attn_out[...] + own_prob * vn[...]
    attended = jnp.concatenate([attn_out[pl.ds(h, R, stride=8), :] for h in range(HEADS)], axis=1).astype(BF16)

    for cp in w_copies + wd_copies:
        cp.start()

    def pack(v):
        return jnp.concatenate([v[:, :384], v[:, 384:]], axis=0).astype(BF16)

    def unpack(v):
        v = v.astype(F32)
        return jnp.concatenate([v[:R], v[R:]], axis=1)

    own_term = None
    for j in (2, 1, 3, 0):
        op_copies[j].wait()
        term = jnp.dot(attended, op_buf[j], preferred_element_type=F32)
        halves = [
            jnp.concatenate([term[:, s * 512 + h * W : s * 512 + (h + 1) * W] for s in range(3)], axis=1)
            for h in range(2)
        ]
        if j:
            for h in range(2):
                z_send[j, h] = pack(halves[h])
                send(z_send.at[j, h], z_recv.at[j, c], ("zs", j, h), device(c=h, z=j), z_sem[j] + c)
        else:
            hidden[0] = halves[0]
            hidden[1] = halves[1]
            own_term = hidden[c]
            z_send[0, 0] = pack(hidden[other])
            send(z_send.at[0, 0], z_recv.at[0, c], ("zs", 0, 0), sibling, z_sem[0] + c)

    for j in (1, 3, 2):
        arrived(info.at[c, me["y"], wrap(me["x"] - j)], ("info x", j))
    for j in (1, 3, 2):
        spot = info.at[c, me["y"]]
        send(spot, spot, ("info y", j), device(y=j))

    acc_g[...] = jnp.zeros_like(acc_g)
    acc_u[...] = jnp.zeros_like(acc_u)
    ssum[...] = jnp.zeros_like(ssum)

    arrived(res_recv, ("res",))
    mine = own_term + res_part(c)
    theirs = res_recv[...]
    arrived(z_recv.at[0, other], None, z_sem[0] + other)
    theirs = theirs + unpack(z_recv[0, other])
    for j in (1, 3, 2):
        for k in range(2):
            arrived(z_recv.at[j, k], None, z_sem[j] + k)
        mine = mine + unpack(z_recv[j, c])
        theirs = theirs + unpack(z_recv[j, other])
    hidden[c] = mine
    hidden[other] = theirs
    sent = jnp.concatenate([hidden[0], hidden[1]], axis=0).astype(BF16)

    place = [tuple(me[a] for a in axes) for axes in STREAMS]
    for s, (a1, a2, a3) in enumerate(STREAMS):
        p1, p2, p3 = place[s]
        x_all[c, s, p3, p2, p1] = sent[:, s * W : (s + 1) * W]
    for s, (a1, a2, a3) in enumerate(STREAMS):
        p1, p2, p3 = place[s]
        for j in (1, 3, 2):
            spot = x_all.at[c, s, p3, p2, p1]
            send(spot, spot, ("g1", s, j), device(**{a1: j}))

    def row(s, j3, j2, core):
        _, p2, p3 = place[s]
        return x_all.at[core, s, wrap(p3 + j3), wrap(p2 + j2)]

    def share(s, j3, j2):
        spot = row(s, j3, j2, c)
        send(spot, spot, ("gs", s, j3, j2), sibling)

    def out3(s, j2):
        a3 = STREAMS[s][2]
        spot = row(s, 0, j2, c)
        for j in (1, 3):
            send(spot, spot, ("g3", s, j, j2), device(**{a3: j}))
        share(s, 0, j2)

    for s, (a1, a2, a3) in enumerate(STREAMS):
        p1, p2, p3 = place[s]
        for j in (1, 3, 2):
            arrived(x_all.at[c, s, p3, p2, wrap(p1 - j)], ("g1", s, j))
        spot = row(s, 0, 0, c)
        for j in (1, 3, 2):
            send(spot, spot, ("g2", s, j), device(**{a2: j}))
        out3(s, 0)

    def take2(j):
        for s in range(3):
            arrived(row(s, 0, -j, c), ("g2", s, j))
            out3(s, 4 - j)

    def take3(j2):
        for s in range(3):
            a3 = STREAMS[s][2]
            for j in (1, 3):
                spot = row(s, -j, j2, c)
                arrived(spot, ("g3", s, j, j2))
                if j2 in (FORWARD_UP if j == 1 else FORWARD_DOWN):
                    send(spot, spot, ("g4", s, j2), device(**{a3: j}))
                share(s, 4 - j, j2)

    def take4(j2):
        for s in range(3):
            spot = row(s, 2, j2, c)
            arrived(spot, ("g4", s, j2))
            share(s, 2, j2)

    def shared(s, j3):
        for j2 in range(4):
            arrived(row(s, j3, j2, other), ("gs", s, j3, j2))

    def multiply(s, j3):
        q = wrap(place[s][2] + j3)

        def step(i, carry):
            z = q if s == 0 else i
            spot = (i,) if s == 0 else ((slice(None), q) if s == 1 else (q,))
            g = u = sq = None
            for h in range(2):
                if s == 2:
                    x = x_all[h, s, q, :, i]
                else:
                    x = x_all[h, s, q, i]
                x = x.reshape(4 * R2, W).astype(F32)
                k = z * 6 + s * 2 + h
                part_sq = x * x
                part_sq = part_sq[:, :128] + part_sq[:, 128:]
                xb = (x * gain[k]).astype(BF16)
                rows = pl.ds(pl.multiple_of(k * W, W), W)
                part_g = jnp.dot(xb, wg[rows, :], preferred_element_type=F32)
                part_u = jnp.dot(xb, wu[rows, :], preferred_element_type=F32)
                g = part_g if g is None else g + part_g
                u = part_u if u is None else u + part_u
                sq = part_sq if sq is None else sq + part_sq
            acc_g[spot] = acc_g[spot] + g.reshape(4, R2, W)
            acc_u[spot] = acc_u[spot] + u.reshape(4, R2, W)
            ssum[spot] = ssum[spot] + sq.reshape(4, R2, 128)
            return carry

        lax.fori_loop(0, 4, step, 0)

    take2(1)
    take3(0)
    take2(3)
    take3(3)
    take2(2)
    for j in (1, 3, 2):
        arrived(info.at[c, wrap(me["y"] - j)], ("info y", j))
    send(info.at[c], info.at[c], ("info c",), sibling)
    for cp in w_copies + wd_copies:
        cp.wait()
    for s in range(3):
        shared(s, 0)
        multiply(s, 0)
    take3(1)
    take3(2)
    take4(0)
    for s in range(3):
        for j3 in (1, 3):
            shared(s, j3)
            multiply(s, j3)
    take4(3)
    take4(1)
    take4(2)
    arrived(info.at[other], ("info c",))
    for s in range(3):
        shared(s, 2)
        multiply(s, 2)

    lane4 = lax.broadcasted_iota(jnp.int32, (4, R2, 128), 2)

    def activate(i, carry):
        both = jnp.concatenate([info[0, i], info[1, i]], axis=1)
        chosen = jnp.sum(jnp.where(lane4 == me["x"], both, 0.0), axis=2, keepdims=True)
        inv = lax.rsqrt(jnp.sum(ssum[i], axis=2, keepdims=True) / D + 1e-05)
        g = acc_g[i] * inv
        u = acc_u[i] * inv
        act[i] = (g / (1.0 + jnp.exp(-g)) * u * chosen).astype(BF16)
        return carry

    lax.fori_loop(0, 4, activate, 0)

    def down(s, j3, half, store):
        q = wrap(place[s][2] + j3)

        def step(i, carry):
            if s == 0:
                a, w = act[i], wd[half, q, s]
            elif s == 1:
                a, w = act[:, q], wd[half, i, s]
            else:
                a, w = act[q], wd[half, i, s]
            y = jnp.dot(a.reshape(4 * R2, W), w, preferred_element_type=F32).reshape(4, R2, W)
            store(y, (slice(None), i) if s == 2 else (i,))
            return carry

        lax.fori_loop(0, 4, step, 0)

    def for_sibling(s, j3):
        def store(y, spot):
            sib_out[(s, j3) + spot] = y.astype(BF16)

        down(s, j3, 1, store)
        send(sib_out.at[s, j3], sib_in.at[s, j3], ("rs", s, j3), sibling)

    def for_chip(s, j3):
        arrived(sib_in.at[s, j3], ("rs", s, j3))

        def store(y, spot):
            part[(s, j3) + spot] = (y + sib_in[(s, j3) + spot].astype(F32)).astype(BF16)

        down(s, j3, 0, store)

    def second(s, j2):
        return wrap(place[s][1] + j2)

    def send_far(s):
        a3 = STREAMS[s][2]
        for j, rows in ((1, FORWARD_UP), (3, FORWARD_DOWN)):
            for j2 in rows:
                r = second(s, j2)
                send(part.at[s, 2, r], d2_in.at[s, r], ("r4", s, j2), device(**{a3: j}))

    def send_near(s, j, j2):
        r = second(s, j2)
        send(part.at[s, j, r], plane_in.at[s, j // 2, r], ("r3", s, j, j2), device(**{STREAMS[s][2]: j}))

    for s in range(3):
        for_sibling(s, 2)
    for s in range(3):
        for_sibling(s, 1)
        for_chip(s, 2)
        send_far(s)
    for s in range(3):
        for_sibling(s, 3)
        for_chip(s, 1)
        for j2 in FORWARD_DOWN:
            send_near(s, 1, j2)
    for s in range(3):
        for_sibling(s, 0)
        for_chip(s, 3)
        for j2 in FORWARD_UP:
            send_near(s, 3, j2)
    for s in range(3):
        for_chip(s, 0)
    drain()
    for j2 in (2, 3, 1, 0):
        j = 1 if j2 in FORWARD_UP else 3
        for s in range(3):
            r = second(s, j2)
            arrived(d2_in.at[s, r], ("r4", s, j2))
            part[s, j, r] = (part[s, j, r].astype(F32) + d2_in[s, r].astype(F32)).astype(BF16)
            send_near(s, j, j2)

    for j2 in (2, 3, 1, 0):
        for s in range(3):
            r = second(s, j2)
            for j in (1, 3):
                arrived(plane_in.at[s, j // 2, r], ("r3", s, j, j2))
            v = part[s, 0, r].astype(F32) + plane_in[s, 0, r].astype(F32) + plane_in[s, 1, r].astype(F32)
            if j2:
                row_out[s, j2 - 1] = v.astype(BF16)
                send(row_out.at[s, j2 - 1], row_in.at[s, j2 - 1], ("r2", s, j2), device(**{STREAMS[s][1]: j2}))
            else:
                row_own[s] = v
    for s in range(3):
        v = row_own[s]
        for j2 in (1, 2, 3):
            arrived(row_in.at[s, j2 - 1], ("r2", s, j2))
            v = v + row_in[s, j2 - 1].astype(F32)
        row_own[s] = v
        for j1 in (2, 1, 3):
            blk_out[s, j1 - 1] = row_own[s, wrap(place[s][0] + j1)].astype(BF16)
            send(blk_out.at[s, j1 - 1], blk_in.at[s, j1 - 1], ("r1", s, j1), device(**{STREAMS[s][0]: j1}))
    for s in range(3):
        v = row_own[s, place[s][0]]
        for j1 in (1, 2, 3):
            arrived(blk_in.at[s, j1 - 1], ("r1", s, j1))
            v = v + blk_in[s, j1 - 1].astype(F32)
        for k in range(2):
            hidden[k, :, s * W : (s + 1) * W] = hidden[k, :, s * W : (s + 1) * W] + v[k * R : (k + 1) * R]
    fin_send[...] = hidden[other]
    send(fin_send, fin.at[c], ("fin",), sibling)
    fin[c] = hidden[c]
    drain()
    arrived(fin.at[other], ("fin",))
    for s in range(3):
        for h in range(2):
            out[:, s * 512 + h * W : s * 512 + (h + 1) * W] = fin[h, :, s * W : (s + 1) * W].astype(BF16)


def local_step(
    new_query, new_kv, kv_cache, lengths, residual, out_proj, expert_ids, gate_weights, slot_expert, moe_gain,
    w_gate, w_up, w_down,
):
    vmem = pl.BlockSpec(memory_space=pltpu.VMEM)
    smem = pl.BlockSpec(memory_space=pltpu.SMEM)
    anywhere = pl.BlockSpec(memory_space=pl.ANY)
    v = pltpu.VMEM
    return pl.pallas_call(
        kernel,
        out_shape=jax.ShapeDtypeStruct((R, QD), BF16),
        in_specs=[smem, smem] + [vmem] * 6 + [anywhere] * 5,
        out_specs=vmem,
        scratch_shapes=[
            v((R, CACHE, HD), BF16),
            v((R, CACHE, HD), BF16),
            v((4, HEADS * HD, QD), BF16),
            v((D, W), BF16),
            v((D, W), BF16),
            v((2, 4, 3, W, W), BF16),
            v((R * 8, HD), F32),
            v((R * 8, HD), F32),
            v((R * 8, HD), F32),
            v((R * 8, CACHE), F32),
            v((R * 8, HD), F32),
            v((2, 4, 4, R, 128), F32),
            v((R, 3 * W), F32),
            v((R, 3 * W), F32),
            v((4, 2, R2, 384), BF16),
            v((4, 2, R2, 384), BF16),
            v((2, R, 3 * W), F32),
            v((2, 3, 4, 4, 4, R2, W), BF16),
            v((4, 4, R2, 128), F32),
            v((4, 4, R2, W), F32),
            v((4, 4, R2, W), F32),
            v((4, 4, R2, W), BF16),
            v((3, 4, 4, 4, R2, W), BF16),
            v((3, 4, 4, 4, R2, W), BF16),
            v((3, 4, 4, 4, R2, W), BF16),
            v((3, 4, 4, R2, W), BF16),
            v((3, 2, 4, 4, R2, W), BF16),
            v((3, 3, 4, R2, W), BF16),
            v((3, 3, 4, R2, W), BF16),
            v((3, 4, R2, W), F32),
            v((3, 3, R2, W), BF16),
            v((3, 3, R2, W), BF16),
            v((R, 3 * W), F32),
            v((2, R, 3 * W), F32),
            pltpu.SemaphoreType.DMA((SEMS,)),
            pltpu.SemaphoreType.DMA((SEMS,)),
            pltpu.SemaphoreType.DMA((38,)),
        ],
        compiler_params=pltpu.CompilerParams(
            collective_id=0, has_side_effects=True, vmem_limit_bytes=62 * 2**20
        ),
        name="decode_layer",
    )(
        lengths, slot_expert, new_query, new_kv.reshape(R, 2 * HD), residual, expert_ids, gate_weights,
        moe_gain.reshape(D // W, 1, W), kv_cache, out_proj, w_gate, w_up, w_down,
    )


def solution(mesh):
    placed = (
        P(("attn", "exp"), "tp"),
        P(("attn", "exp"), None, "tp"),
        P(("attn", "exp"), None, None, "tp"),
        P(("attn", "exp")),
        P(("attn", "exp"), None),
        P("tp", None),
        P(("attn", "exp"), None),
        P(("attn", "exp"), None),
        P(),
        P(),
        P("exp", None, ("attn", "tp")),
        P("exp", None, ("attn", "tp")),
        P("exp", ("attn", "tp"), None),
    )
    return jax.shard_map(
        local_step, mesh=mesh, in_specs=placed, out_specs=P(("attn", "exp"), "tp"), check_vma=False
    )
```

```python
import jax
import jax.numpy as jnp
from jax import lax
from jax.experimental import pallas as pl
from jax.experimental.pallas import tpu as pltpu
from jax.sharding import PartitionSpec as P

MESH = pl.DeviceIdType.MESH
F32 = jnp.float32
BF16 = jnp.bfloat16

HD = 128
HEADS = 6
R = 24
R2 = 48
CACHE = 512
D = 6144
QD = 1536
W = 256
SEMS = 93
SENDS = 18

STREAMS = (("x", "y", "z"), ("y", "z", "x"), ("z", "x", "y"))
FORWARD_UP = (0, 3)
FORWARD_DOWN = (1, 2)


def wrap(v):
    return lax.rem(v + 4, 4)


def kernel(
    lengths, slot_expert, query, new_kv, residual, ids, gate_w, gain, cache, out_proj, w_gate, w_up, w_down,
    out,
    k_buf, v_buf, op_buf, wg, wu, wd, q_pad, kn, vn, scores, attn_out,
    info_pad, info, res_send, res_recv, z_send, z_recv, z_sib, hidden,
    x_all, ssum, acc_g, acc_u, act,
    part, d2_in, plane_in, row_out, row_in, row_own, blk_out, blk_in, fin_send, fin,
    send_sems, recv_sems, local_sems,
):
    attn = lax.axis_index("attn")
    me = {"y": attn // 2, "c": lax.rem(attn, 2), "z": lax.axis_index("tp"), "x": lax.axis_index("exp")}
    c, other = me["c"], 1 - me["c"]

    def device(c=None, **steps):
        at = dict(me)
        for axis, step in steps.items():
            at[axis] = wrap(at[axis] + step)
        if c is not None:
            at["c"] = c
        return (at["y"] * 2 + at["c"], at["z"], at["x"])

    sibling = device(c=other)

    def local(src, dst, i):
        return pltpu.make_async_copy(src, dst, local_sems.at[i])

    k_copies = [local(cache.at[pl.ds(i * 6, 6), 0], k_buf.at[pl.ds(i * 6, 6)], i) for i in range(4)]
    v_copies = [local(cache.at[pl.ds(i * 6, 6), 1], v_buf.at[pl.ds(i * 6, 6)], 4 + i) for i in range(4)]
    op_copies = {
        j: local(out_proj.at[:, pl.ds(pl.multiple_of(wrap(me["z"] + j) * QD, QD), QD)], op_buf.at[j], 8 + j)
        for j in (2, 1, 3, 0)
    }
    w_copies = [local(w_gate.at[0], wg, 12), local(w_up.at[0], wu, 13)]

    def down_columns(z, s, h):
        return w_down.at[0, :, pl.ds(pl.multiple_of(z * QD + s * 512 + h * W, W), W)]

    def down_rows(core):
        return pl.ds(pl.multiple_of(core * W, W), W)

    for cp in k_copies + v_copies:
        cp.start()
    for j in (2, 1, 3, 0):
        op_copies[j].start()

    barrier = pltpu.get_barrier_semaphore()
    partners = [device(c=k, z=j) for j in (1, 2, 3) for k in (0, 1)] + [sibling]
    partners += [device(**{a: j}) for a in ("x", "y") for j in (1, 2, 3)]
    for p in partners:
        pl.semaphore_signal(barrier, inc=1, device_id=p, device_id_type=MESH)

    table, classes = {}, {}

    def sem(key):
        if key not in table:
            table[key] = len(table)
            assert len(table) <= SEMS
        return recv_sems.at[table[key]]

    def left(kind):
        if kind not in classes:
            classes[kind] = len(classes)
            assert len(classes) <= SENDS
        return send_sems.at[classes[kind]]

    def send(src, dst, kind, key, to):
        pltpu.make_async_remote_copy(
            src_ref=src, dst_ref=dst, send_sem=left(kind), recv_sem=sem(key), device_id=to, device_id_type=MESH
        ).start()

    def arrived(dst, key):
        pltpu.make_async_remote_copy(
            src_ref=dst, dst_ref=dst, send_sem=send_sems.at[0], recv_sem=sem(key),
            device_id=sibling, device_id_type=MESH,
        ).wait_recv()

    def drain(src, kind):
        pltpu.make_async_remote_copy(
            src_ref=src, dst_ref=src, send_sem=left(kind), recv_sem=recv_sems.at[0],
            device_id=sibling, device_id_type=MESH,
        ).wait_send()

    info_pad[...] = jnp.zeros_like(info_pad)
    for s in range(4):
        hit = jnp.where(ids[...] == slot_expert[s], gate_w[...], 0.0)
        info_pad[s : s + 1, :R] = jnp.sum(hit, axis=0, keepdims=True)
    info[c, me["y"], me["x"]] = info_pad[...].T[:R]

    def res_part(h):
        return jnp.concatenate(
            [residual[:, pl.ds(pl.multiple_of(me["z"] * QD + s * 512 + h * W, W), W)] for s in range(3)], axis=1
        ).astype(F32)

    res_send[...] = res_part(other)

    for h in range(8):
        if h < HEADS:
            q_pad[pl.ds(h, R, stride=8), :] = query[:, h * HD : (h + 1) * HD].astype(F32)
        else:
            q_pad[pl.ds(h, R, stride=8), :] = jnp.zeros((R, HD), F32)
        kn[pl.ds(h, R, stride=8), :] = new_kv[:, 0, :].astype(F32)
        vn[pl.ds(h, R, stride=8), :] = new_kv[:, 1, :].astype(F32)
    scale = HD ** (-0.5)
    position = lax.broadcasted_iota(jnp.int32, (8, CACHE), 1)

    for i in range(4):
        k_copies[i].wait()
        for r in range(i * 6, i * 6 + 6):
            s = lax.dot_general(
                q_pad[r * 8 : r * 8 + 8, :].astype(BF16), k_buf[r], (((1,), (1,)), ((), ())),
                preferred_element_type=F32,
            ) * scale
            scores[r * 8 : r * 8 + 8, :] = jnp.where(position < lengths[r], s, -1e30)
    own_score = jnp.sum(q_pad[...] * kn[...], axis=1, keepdims=True) * scale
    raw = scores[...]
    top = jnp.maximum(jnp.max(raw, axis=1, keepdims=True), own_score)
    weight = jnp.exp(raw - top)
    own_weight = jnp.exp(own_score - top)
    total = jnp.sum(weight, axis=1, keepdims=True) + own_weight
    scores[...] = weight / total
    own_prob = (own_weight / total).astype(BF16).astype(F32)
    for i in range(4):
        v_copies[i].wait()
        for r in range(i * 6, i * 6 + 6):
            attn_out[r * 8 : r * 8 + 8, :] = jnp.dot(
                scores[r * 8 : r * 8 + 8, :].astype(BF16), v_buf[r], preferred_element_type=F32
            )
    attn_out[...] = attn_out[...] + own_prob * vn[...]
    attended = jnp.concatenate([attn_out[pl.ds(h, R, stride=8), :] for h in range(HEADS)], axis=1).astype(BF16)

    def pack(v):
        return jnp.concatenate([v[:, :384], v[:, 384:]], axis=0).astype(BF16)

    def unpack(v):
        v = v.astype(F32)
        return jnp.concatenate([v[:R], v[R:]], axis=1)

    own_term = None
    for j in (2, 1, 3, 0):
        op_copies[j].wait()
        term = jnp.dot(attended, op_buf[j], preferred_element_type=F32)
        halves = [
            jnp.concatenate([term[:, s * 512 + h * W : s * 512 + (h + 1) * W] for s in range(3)], axis=1)
            for h in range(2)
        ]
        if j == 2:
            pl.semaphore_wait(barrier, len(partners))
            send(res_send, res_recv, "res", "res", sibling)
        if j:
            for h in range(2):
                z_send[j - 1, h] = pack(halves[h])
                send(z_send.at[j - 1, h], z_recv.at[j - 1, c], "z", "z", device(c=h, z=j))
        else:
            hidden[0] = halves[0]
            hidden[1] = halves[1]
            own_term = hidden[c]
            z_sib[0] = pack(hidden[other])
            send(z_sib.at[0], z_sib.at[1], "zs", "zs", sibling)

    for cp in w_copies:
        cp.start()
    for j in (1, 3, 2):
        spot = info.at[c, me["y"], me["x"]]
        send(spot, spot, "ix", "ix", device(x=j))
    for z in range(4):
        for s in range(3):
            send(down_columns(z, s, other), wd.at[z, s, down_rows(c)], "wd", "wd", sibling)
            local(down_columns(z, s, c), wd.at[z, s, down_rows(c)], 14).start()

    acc_g[...] = jnp.zeros_like(acc_g)
    acc_u[...] = jnp.zeros_like(acc_u)
    ssum[...] = jnp.zeros_like(ssum)

    arrived(res_recv, "res")
    arrived(z_sib.at[1], "zs")
    mine = own_term + res_part(c)
    theirs = res_recv[...] + unpack(z_sib[1])
    arrived(z_recv, "z")
    for j in range(3):
        mine = mine + unpack(z_recv[j, c])
        theirs = theirs + unpack(z_recv[j, other])
    hidden[c] = mine
    hidden[other] = theirs
    sent = jnp.concatenate([hidden[0], hidden[1]], axis=0).astype(BF16)

    place = [tuple(me[a] for a in axes) for axes in STREAMS]

    def own_blocks(core, s, n):
        return x_all.at[core, s, 0, 0, pl.ds(0, n)]

    for s, (a1, a2, a3) in enumerate(STREAMS):
        p1, p2, p3 = place[s]
        x_all[c, s, p3, p2, p1] = sent[:, s * W : (s + 1) * W]
        for j in (1, 3, 2):
            spot = x_all.at[c, s, p3, p2, p1]
            send(spot, spot, "g1", ("g1", s), device(**{a1: j}))

    def row(s, j3, j2, core):
        _, p2, p3 = place[s]
        return x_all.at[core, s, wrap(p3 + j3), wrap(p2 + j2)]

    def share_key(s, j3, j2):
        if j3 == 0:
            return ("gs", s, 0, j2 == 0)
        if j3 == 2:
            return ("gs", s, 2, j2 == 2)
        return ("gs", s, 1, j2 in (0, 1))

    def share(s, j3, j2):
        spot = row(s, j3, j2, c)
        send(spot, spot, "gs", share_key(s, j3, j2), sibling)

    def shared(j3, j2):
        for s in range(3):
            key = share_key(s, j3, j2)
            if j3 == 1:
                size = x_all.at[other, s, 0]
            elif key[3]:
                size = x_all.at[other, s, 0, 0]
            else:
                size = x_all.at[other, s, 0, pl.ds(0, 3)]
            arrived(size, key)

    def out3(s, j2):
        spot = row(s, 0, j2, c)
        for j in (1, 3):
            send(spot, spot, "g3", ("g3", s, j2), device(**{STREAMS[s][2]: j}))
        share(s, 0, j2)

    def take1():
        for s, (a1, a2, a3) in enumerate(STREAMS):
            arrived(x_all.at[c, s, 0, 0, pl.ds(0, 3)], ("g1", s))
            spot = row(s, 0, 0, c)
            for j in (1, 3, 2):
                send(spot, spot, "g2", ("g2", s, j), device(**{a2: j}))
            out3(s, 0)

    def take2(j):
        for s in range(3):
            arrived(row(s, 0, -j, c), ("g2", s, j))
            out3(s, 4 - j)

    def take3(j2):
        for s in range(3):
            arrived(x_all.at[c, s, 0, pl.ds(0, 2)], ("g3", s, j2))
            for j in (1, 3):
                spot = row(s, -j, j2, c)
                if j2 in (FORWARD_UP if j == 1 else FORWARD_DOWN):
                    send(spot, spot, "g3", ("g4", s, j2), device(**{STREAMS[s][2]: j}))
                share(s, 4 - j, j2)

    def take4(j2):
        for s in range(3):
            spot = row(s, 2, j2, c)
            arrived(spot, ("g4", s, j2))
            share(s, 2, j2)

    def multiply(xs, k0, spot):
        g = u = sq = None
        for h in range(2):
            x = xs[h].reshape(4 * R2, W).astype(F32)
            k = k0 + h
            part_sq = x * x
            part_sq = part_sq[:, :128] + part_sq[:, 128:]
            xb = (x * gain[k]).astype(BF16)
            rows = pl.ds(pl.multiple_of(k * W, W), W)
            part_g = jnp.dot(xb, wg[rows, :], preferred_element_type=F32)
            part_u = jnp.dot(xb, wu[rows, :], preferred_element_type=F32)
            g = part_g if g is None else g + part_g
            u = part_u if u is None else u + part_u
            sq = part_sq if sq is None else sq + part_sq
        acc_g[spot] = acc_g[spot] + g.reshape(4, R2, W)
        acc_u[spot] = acc_u[spot] + u.reshape(4, R2, W)
        ssum[spot] = ssum[spot] + sq.reshape(4, R2, 128)

    def rows_01(count, at):
        def step(t, carry):
            j3, j2 = at(t)
            for s in range(2):
                q, i = wrap(place[s][2] + j3), wrap(place[s][1] + j2)
                xs = [x_all[h, s, q, i] for h in range(2)]
                multiply(xs, (q if s == 0 else i) * 6 + s * 2, (i,) if s == 0 else (slice(None), q))
            return carry

        lax.fori_loop(0, count, step, 0)

    def planes_2(count, at):
        def step(t, carry):
            q, i = wrap(place[2][2] + at(t // 4)), lax.rem(t, 4)
            xs = [x_all[h, 2, q, :, i] for h in range(2)]
            multiply(xs, i * 6 + 4, (q,))
            return carry

        lax.fori_loop(0, 4 * count, step, 0)

    take1()
    for cp in w_copies:
        cp.wait()
    shared(0, 0)
    rows_01(1, lambda t: (0, 0))
    take2(1)
    take2(3)
    take2(2)
    take3(0)
    arrived(info.at[c, 0, pl.ds(0, 3)], "ix")
    for j in (1, 3, 2):
        spot = info.at[c, me["y"]]
        send(spot, spot, "iy", "iy", device(y=j))
    shared(0, 1)
    rows_01(2, lambda t: (0, 1 + 2 * t))
    take3(1)
    rows_01(1, lambda t: (0, 2))
    planes_2(1, lambda n: 0)
    take3(3)
    shared(1, 0)
    rows_01(4, lambda t: (1 + 2 * lax.rem(t, 2), t // 2))
    take3(2)
    take4(0)
    take4(1)
    arrived(info.at[c, pl.ds(0, 3)], "iy")
    send(info.at[c], info.at[c], "ic", "ic", sibling)
    shared(1, 3)
    rows_01(4, lambda t: (1 + 2 * lax.rem(t, 2), 3 - t // 2))
    take4(3)
    planes_2(2, lambda n: 1 + 2 * n)
    take4(2)
    shared(2, 0)
    rows_01(3, lambda t: (2, t + t // 2))
    shared(2, 2)
    rows_01(1, lambda t: (2, 2))
    planes_2(1, lambda n: 2)

    arrived(info.at[other], "ic")
    lane4 = lax.broadcasted_iota(jnp.int32, (4, R2, 128), 2)

    def activate(i, carry):
        both = jnp.concatenate([info[0, i], info[1, i]], axis=1)
        chosen = jnp.sum(jnp.where(lane4 == me["x"], both, 0.0), axis=2, keepdims=True)
        inv = lax.rsqrt(jnp.sum(ssum[i], axis=2, keepdims=True) / D + 1e-05)
        g = acc_g[i] * inv
        u = acc_u[i] * inv
        act[c, i] = (g / (1.0 + jnp.exp(-g)) * u * chosen).astype(BF16)
        send(act.at[c, i], act.at[c, i], "act", "act", sibling)
        return carry

    lax.fori_loop(0, 4, activate, 0)
    local(wd.at[:, :, down_rows(0)], wd.at[:, :, down_rows(0)], 14).wait()
    arrived(wd.at[:, :, down_rows(0)], "wd")
    arrived(act.at[other], "act")

    def down(s, j3):
        q = wrap(place[s][2] + j3)

        def step(i, carry):
            pick = (i,) if s == 0 else ((slice(None), q) if s == 1 else (q,))
            a = jnp.concatenate([act[(h,) + pick].reshape(4 * R2, W) for h in range(2)], axis=1)
            w = wd[q if s == 0 else i, s]
            y = jnp.dot(a, w, preferred_element_type=F32).reshape(4, R2, W).astype(BF16)
            if s == 2:
                part[s, j3, :, i] = y
            else:
                part[s, j3, i] = y
            return carry

        lax.fori_loop(0, 4, step, 0)

    def second(s, j2):
        return wrap(place[s][1] + j2)

    def send_far(s):
        for j2 in (2, 3, 1, 0):
            j = 1 if j2 in FORWARD_UP else 3
            r = second(s, j2)
            send(part.at[s, 2, r], d2_in.at[s, r], "r4", ("r4", s, j2), device(**{STREAMS[s][2]: j}))

    def send_near(s, j, j2):
        r = second(s, j2)
        send(part.at[s, j, r], plane_in.at[s, j // 2, r], "r3", ("r3", s, j2), device(**{STREAMS[s][2]: j}))

    for s in range(3):
        down(s, 2)
        send_far(s)
    for s in range(3):
        down(s, 1)
        for j2 in (2, 1):
            send_near(s, 1, j2)
        down(s, 3)
        for j2 in (3, 0):
            send_near(s, 3, j2)
    for s in range(3):
        down(s, 0)
    for j2 in (2, 3, 1, 0):
        j = 1 if j2 in FORWARD_UP else 3
        for s in range(3):
            r = second(s, j2)
            arrived(d2_in.at[s, r], ("r4", s, j2))
            part[s, j, r] = (part[s, j, r].astype(F32) + d2_in[s, r].astype(F32)).astype(BF16)
            send_near(s, j, j2)

    for j2 in (2, 3, 1, 0):
        for s in range(3):
            r = second(s, j2)
            arrived(plane_in.at[s, :, r], ("r3", s, j2))
            v = part[s, 0, r].astype(F32) + plane_in[s, 0, r].astype(F32) + plane_in[s, 1, r].astype(F32)
            if j2:
                row_out[s, j2 - 1] = v.astype(BF16)
                send(row_out.at[s, j2 - 1], row_in.at[s, j2 - 1], "r2", ("r2", s), device(**{STREAMS[s][1]: j2}))
            else:
                row_own[s] = v
    for s in range(3):
        arrived(row_in.at[s], ("r2", s))
        row_own[s] = row_own[s] + (
            row_in[s, 0].astype(F32) + row_in[s, 1].astype(F32) + row_in[s, 2].astype(F32)
        )
        for j1 in (2, 1, 3):
            blk_out[s, j1 - 1] = row_own[s, wrap(place[s][0] + j1)].astype(BF16)
            send(blk_out.at[s, j1 - 1], blk_in.at[s, j1 - 1], "r1", ("r1", s), device(**{STREAMS[s][0]: j1}))

    drain(res_send, "res")
    drain(z_send, "z")
    drain(z_sib.at[0], "zs")
    drain(info.at[c, 0, pl.ds(0, 3)], "ix")
    drain(info.at[c, pl.ds(0, 3)], "iy")
    drain(info.at[c], "ic")
    drain(wd.at[:, :, down_rows(0)], "wd")
    drain(x_all.at[c, :, 0, 0, pl.ds(0, 3)], "g1")
    drain(x_all.at[c, :, 0, pl.ds(0, 3)], "g2")
    drain(x_all.at[c, :, pl.ds(0, 3)], "g3")
    drain(x_all.at[c], "gs")
    drain(act.at[c], "act")
    drain(d2_in, "r4")
    drain(plane_in, "r3")
    drain(row_out, "r2")

    for s in range(3):
        v = row_own[s, place[s][0]]
        arrived(blk_in.at[s], ("r1", s))
        for j in range(3):
            v = v + blk_in[s, j].astype(F32)
        for k in range(2):
            fin_send[k, s] = hidden[k, :, s * W : (s + 1) * W] + v[k * R : (k + 1) * R]
        send(fin_send.at[other, s], fin.at[s], "fin", "fin", sibling)
    drain(blk_out, "r1")
    arrived(fin, "fin")
    drain(fin, "fin")
    for s in range(3):
        fin_send[other, s] = fin[s]
        for h in range(2):
            out[:, s * 512 + h * W : s * 512 + (h + 1) * W] = fin_send[h, s].astype(BF16)


def local_step(
    new_query, new_kv, kv_cache, lengths, residual, out_proj, expert_ids, gate_weights, slot_expert, moe_gain,
    w_gate, w_up, w_down,
):
    vmem = pl.BlockSpec(memory_space=pltpu.VMEM)
    smem = pl.BlockSpec(memory_space=pltpu.SMEM)
    anywhere = pl.BlockSpec(memory_space=pl.ANY)
    v = pltpu.VMEM
    return pl.pallas_call(
        kernel,
        out_shape=jax.ShapeDtypeStruct((R, QD), BF16),
        in_specs=[smem, smem] + [vmem] * 6 + [anywhere] * 5,
        out_specs=vmem,
        scratch_shapes=[
            v((R, CACHE, HD), BF16),
            v((R, CACHE, HD), BF16),
            v((4, HEADS * HD, QD), BF16),
            v((D, W), BF16),
            v((D, W), BF16),
            v((4, 3, 2 * W, W), BF16),
            v((R * 8, HD), F32),
            v((R * 8, HD), F32),
            v((R * 8, HD), F32),
            v((R * 8, CACHE), F32),
            v((R * 8, HD), F32),
            v((128, 128), F32),
            v((2, 4, 4, R, 128), F32),
            v((R, 3 * W), F32),
            v((R, 3 * W), F32),
            v((3, 2, R2, 384), BF16),
            v((3, 2, R2, 384), BF16),
            v((2, R2, 384), BF16),
            v((2, R, 3 * W), F32),
            v((2, 3, 4, 4, 4, R2, W), BF16),
            v((4, 4, R2, 128), F32),
            v((4, 4, R2, W), F32),
            v((4, 4, R2, W), F32),
            v((2, 4, 4, R2, W), BF16),
            v((3, 4, 4, 4, R2, W), BF16),
            v((3, 4, 4, R2, W), BF16),
            v((3, 2, 4, 4, R2, W), BF16),
            v((3, 3, 4, R2, W), BF16),
            v((3, 3, 4, R2, W), BF16),
            v((3, 4, R2, W), F32),
            v((3, 3, R2, W), BF16),
            v((3, 3, R2, W), BF16),
            v((2, 3, R, W), F32),
            v((3, R, W), F32),
            pltpu.SemaphoreType.DMA((SENDS,)),
            pltpu.SemaphoreType.DMA((SEMS,)),
            pltpu.SemaphoreType.DMA((15,)),
        ],
        compiler_params=pltpu.CompilerParams(
            collective_id=0, has_side_effects=True, vmem_limit_bytes=62 * 2**20
        ),
        name="decode_layer",
    )(
        lengths, slot_expert, new_query, new_kv, residual, expert_ids.T, gate_weights.T,
        moe_gain.reshape(D // W, 1, W), kv_cache, out_proj, w_gate, w_up, w_down,
    )


def solution(mesh):
    placed = (
        P(("attn", "exp"), "tp"),
        P(("attn", "exp"), None, "tp"),
        P(("attn", "exp"), None, None, "tp"),
        P(("attn", "exp")),
        P(("attn", "exp"), None),
        P("tp", None),
        P(("attn", "exp"), None),
        P(("attn", "exp"), None),
        P(),
        P(),
        P("exp", None, ("attn", "tp")),
        P("exp", None, ("attn", "tp")),
        P("exp", ("attn", "tp"), None),
    )
    return jax.shard_map(
        local_step, mesh=mesh, in_specs=placed, out_specs=P(("attn", "exp"), "tp"), check_vma=False
    )
```

```python
import jax
import jax.numpy as jnp
from jax import lax
from jax.experimental import pallas as pl
from jax.experimental.pallas import tpu as pltpu
from jax.sharding import PartitionSpec as P

MESH = pl.DeviceIdType.MESH
F32 = jnp.float32
BF16 = jnp.bfloat16

HD = 128
HEADS = 6
R = 24
CACHE = 512
D = 6144
QD = 1536
W = 256
SEMS = 44
SENDS = 20
PARTS = ((0, R),)
CHUNK = 6

STREAMS = (("x", "y", "z"), ("y", "z", "x"), ("z", "x", "y"))
FORWARD_UP = (0, 3)
FORWARD_DOWN = (1, 2)


def wrap(v):
    return lax.rem(v + 4, 4)


def common_scratch():
    v = pltpu.VMEM
    return dict(
        k_buf=v((R, CACHE, HD), BF16),
        v_buf=v((R, CACHE, HD), BF16),
        op_buf=v((4, HEADS * HD, QD), BF16),
        wg=v((D, W), BF16),
        wu=v((D, W), BF16),
        wd=v((4, 3, 2 * W, W), BF16),
        q_pad=v((R * 8, HD), F32),
        kn=v((R * 8, HD), F32),
        vn=v((R * 8, HD), F32),
        scores=v((R * 8, CACHE), F32),
        attn_out=v((R * 8, HD), F32),
        info_pad=v((128, 128), F32),
        info=v((2, 4, 4, R, 128), F32),
        res_send=v((R, 3 * W), F32),
        res_recv=v((R, 3 * W), F32),
        hidden=v((2, R, 3 * W), F32),
        result=v((R, QD), F32),
        send_sems=pltpu.SemaphoreType.DMA((SENDS,)),
        recv_sems=pltpu.SemaphoreType.DMA((SEMS,)),
        local_sems=pltpu.SemaphoreType.DMA((7 + 2 * (R // CHUNK),)),
    )


def part_scratch(n):
    v, b = pltpu.VMEM, 2 * n
    return dict(
        z_send=v((3, 2, b, 384), BF16),
        z_recv=v((3, 2, b, 384), BF16),
        z_sib=v((2, b, 384), BF16),
        z_own=v((2, n, 3 * W), F32),
        x_all=v((2, 3, 4, 4, 4, b, W), BF16),
        ssum=v((4, 4, b, 128), F32),
        acc_g=v((4, 4, b, W), F32),
        acc_u=v((4, 4, b, W), F32),
        act=v((2, 4, 4, b, W), BF16),
        part=v((3, 4, 4, 4, b, W), BF16),
        d2_in=v((3, 4, 4, b, W), BF16),
        plane_in=v((3, 2, 4, 4, b, W), BF16),
        row_out=v((3, 3, 4, b, W), BF16),
        row_in=v((3, 3, 4, b, W), BF16),
        row_own=v((3, 4, b, W), F32),
        blk_out=v((3, 3, b, W), BF16),
        blk_in=v((3, 3, b, W), BF16),
        fin_send=v((2, 3, n, W), F32),
        fin=v((3, n, W), F32),
    )


def kernel(*refs):
    (lengths, slot_expert, query, new_kv, residual, ids, gate_w, gain, cache, out_proj, w_gate, w_up, w_down, out) = refs[:14]
    names = common_scratch()
    m = dict(zip(names, refs[14:]))
    at = 14 + len(names)
    buffers = []
    for _, n in PARTS:
        names = part_scratch(n)
        buffers.append(dict(zip(names, refs[at:])))
        at += len(names)
    k_buf, v_buf, op_buf, wg, wu, wd = (m[k] for k in ("k_buf", "v_buf", "op_buf", "wg", "wu", "wd"))
    q_pad, kn, vn, scores, attn_out = (m[k] for k in ("q_pad", "kn", "vn", "scores", "attn_out"))
    info, res_send, res_recv, hidden, result = (m[k] for k in ("info", "res_send", "res_recv", "hidden", "result"))
    info_pad, send_sems, recv_sems, local_sems = (m[k] for k in ("info_pad", "send_sems", "recv_sems", "local_sems"))

    attn = lax.axis_index("attn")
    me = {"y": attn // 2, "c": lax.rem(attn, 2), "z": lax.axis_index("tp"), "x": lax.axis_index("exp")}
    c, other = me["c"], 1 - me["c"]
    place = [tuple(me[a] for a in axes) for axes in STREAMS]

    def device(c=None, **steps):
        at = dict(me)
        for axis, step in steps.items():
            at[axis] = wrap(at[axis] + step)
        if c is not None:
            at["c"] = c
        return (at["y"] * 2 + at["c"], at["z"], at["x"])

    sibling = device(c=other)

    def local(src, dst, i):
        return pltpu.make_async_copy(src, dst, local_sems.at[i])

    op_copies = {
        j: local(out_proj.at[:, pl.ds(pl.multiple_of(wrap(me["z"] + j) * QD, QD), QD)], op_buf.at[j], j)
        for j in (2, 1, 3, 0)
    }
    w_copies = [local(w_gate.at[0], wg, 4), local(w_up.at[0], wu, 5)]
    k_copies, v_copies = [], []
    for i in range(R // CHUNK):
        some = pl.ds(i * CHUNK, CHUNK)
        k_copies.append(local(cache.at[some, 0], k_buf.at[some], 7 + 2 * i))
        v_copies.append(local(cache.at[some, 1], v_buf.at[some], 8 + 2 * i))

    def down_columns(z, s, h):
        return w_down.at[0, :, pl.ds(pl.multiple_of(z * QD + s * 512 + h * W, W), W)]

    def down_rows(core):
        return pl.ds(pl.multiple_of(core * W, W), W)

    for cp in k_copies + v_copies:
        cp.start()
    for j in (2, 1, 3, 0):
        op_copies[j].start()

    barrier = pltpu.get_barrier_semaphore()
    partners = [device(c=k, z=j) for j in (1, 2, 3) for k in (0, 1)] + [sibling]
    partners += [device(**{a: j}) for a in ("x", "y") for j in (1, 2, 3)]
    for p in partners:
        pl.semaphore_signal(barrier, inc=1, device_id=p, device_id_type=MESH)

    table, classes = {}, {}

    def sem(key):
        if key not in table:
            table[key] = len(table)
            assert len(table) <= SEMS
        return recv_sems.at[table[key]]

    def left(kind):
        if kind not in classes:
            classes[kind] = len(classes)
            assert len(classes) <= SENDS
        return send_sems.at[classes[kind]]

    def send(src, dst, kind, key, to):
        pltpu.make_async_remote_copy(
            src_ref=src, dst_ref=dst, send_sem=left(kind), recv_sem=sem(key), device_id=to, device_id_type=MESH
        ).start()

    def arrived(dst, key):
        pltpu.make_async_remote_copy(
            src_ref=dst, dst_ref=dst, send_sem=send_sems.at[0], recv_sem=sem(key),
            device_id=sibling, device_id_type=MESH,
        ).wait_recv()

    def drain(src, kind):
        pltpu.make_async_remote_copy(
            src_ref=src, dst_ref=src, send_sem=left(kind), recv_sem=recv_sems.at[0],
            device_id=sibling, device_id_type=MESH,
        ).wait_send()

    info_pad[...] = jnp.zeros_like(info_pad)
    for s in range(4):
        hit = jnp.where(ids[...] == slot_expert[s], gate_w[...], 0.0)
        info_pad[s : s + 1, :R] = jnp.sum(hit, axis=0, keepdims=True)
    info[c, me["y"], me["x"]] = info_pad[...].T[:R]

    def res_part(h):
        return jnp.concatenate(
            [residual[:, pl.ds(pl.multiple_of(me["z"] * QD + s * 512 + h * W, W), W)] for s in range(3)], axis=1
        ).astype(F32)

    res_send[...] = res_part(other)
    hidden[c] = res_part(c)
    for h in range(8):
        if h < HEADS:
            q_pad[pl.ds(h, R, stride=8), :] = query[:, h * HD : (h + 1) * HD].astype(F32)
        else:
            q_pad[pl.ds(h, R, stride=8), :] = jnp.zeros((R, HD), F32)
        kn[pl.ds(h, R, stride=8), :] = new_kv[:, 0, :].astype(F32)
        vn[pl.ds(h, R, stride=8), :] = new_kv[:, 1, :].astype(F32)

    def begin_links():
        pl.semaphore_wait(barrier, len(partners))
        send(res_send, res_recv, "res", "res", sibling)

    def info_1():
        for j in (1, 3, 2):
            spot = info.at[c, me["y"], me["x"]]
            send(spot, spot, "ix", "ix", device(x=j))

    def info_2():
        arrived(info.at[c, 0, pl.ds(0, 3)], "ix")
        for j in (1, 3, 2):
            spot = info.at[c, me["y"]]
            send(spot, spot, "iy", "iy", device(y=j))

    def info_3():
        arrived(info.at[c, pl.ds(0, 3)], "iy")
        send(info.at[c], info.at[c], "ic", "ic", sibling)

    def load_weights():
        for cp in w_copies:
            cp.start()
        for z in range(4):
            for s in range(3):
                send(down_columns(z, s, other), wd.at[z, s, down_rows(c)], "wd", "wd", sibling)
                local(down_columns(z, s, c), wd.at[z, s, down_rows(c)], 6).start()

    def pack(v):
        return jnp.concatenate([v[:, :384], v[:, 384:]], axis=0).astype(BF16)

    def flow(t):
        r0, n = PARTS[t]
        b = 2 * n
        p = buffers[t]
        z_send, z_recv, z_sib, z_own = (p[k] for k in ("z_send", "z_recv", "z_sib", "z_own"))
        x_all, ssum, acc_g, acc_u, act = (p[k] for k in ("x_all", "ssum", "acc_g", "acc_u", "act"))
        part, d2_in, plane_in = (p[k] for k in ("part", "d2_in", "plane_in"))
        row_out, row_in, row_own, blk_out, blk_in = (p[k] for k in ("row_out", "row_in", "row_own", "blk_out", "blk_in"))
        fin_send, fin = p["fin_send"], p["fin"]

        scale = HD ** (-0.5)
        position = lax.broadcasted_iota(jnp.int32, (8, CACHE), 1)
        mine8 = slice(r0 * 8, (r0 + n) * 8)
        for r in range(r0, r0 + n):
            if r % CHUNK == 0:
                k_copies[r // CHUNK].wait()
            s = lax.dot_general(
                q_pad[r * 8 : r * 8 + 8, :].astype(BF16), k_buf[r], (((1,), (1,)), ((), ())),
                preferred_element_type=F32,
            ) * scale
            scores[r * 8 : r * 8 + 8, :] = jnp.where(position < lengths[r], s, -1e30)
        own_score = jnp.sum(q_pad[mine8, :] * kn[mine8, :], axis=1, keepdims=True) * scale
        raw = scores[mine8, :]
        top = jnp.maximum(jnp.max(raw, axis=1, keepdims=True), own_score)
        weight = jnp.exp(raw - top)
        own_weight = jnp.exp(own_score - top)
        total = jnp.sum(weight, axis=1, keepdims=True) + own_weight
        scores[mine8, :] = weight / total
        own_prob = (own_weight / total).astype(BF16).astype(F32)
        for r in range(r0, r0 + n):
            if r % CHUNK == 0:
                v_copies[r // CHUNK].wait()
            attn_out[r * 8 : r * 8 + 8, :] = jnp.dot(
                scores[r * 8 : r * 8 + 8, :].astype(BF16), v_buf[r], preferred_element_type=F32
            )
        attn_out[mine8, :] = attn_out[mine8, :] + own_prob * vn[mine8, :]
        attended = jnp.concatenate(
            [attn_out[pl.ds(r0 * 8 + h, n, stride=8), :] for h in range(HEADS)], axis=1
        ).astype(BF16)

        def unpack(v):
            v = v.astype(F32)
            return jnp.concatenate([v[:n], v[n:]], axis=1)

        for j in (2, 1, 3, 0):
            if t == 0:
                op_copies[j].wait()
            term = jnp.dot(attended, op_buf[j], preferred_element_type=F32)
            halves = [
                jnp.concatenate([term[:, s * 512 + h * W : s * 512 + (h + 1) * W] for s in range(3)], axis=1)
                for h in range(2)
            ]
            if j == 2 and t == 0:
                begin_links()
            if j:
                for h in range(2):
                    z_send[j - 1, h] = pack(halves[h])
                    send(z_send.at[j - 1, h], z_recv.at[j - 1, c], ("z", t), ("z", t), device(c=h, z=j))
            else:
                z_own[0] = halves[0]
                z_own[1] = halves[1]
                z_sib[0] = pack(z_own[other])
                send(z_sib.at[0], z_sib.at[1], ("zs", t), ("zs", t), sibling)
        info_1()
        load_weights()
        acc_g[...] = jnp.zeros_like(acc_g)
        acc_u[...] = jnp.zeros_like(acc_u)
        ssum[...] = jnp.zeros_like(ssum)

        def pass_on(s, j):
            p1, p2, p3 = place[s]
            spot = x_all.at[c, s, p3, p2, wrap(p1 - j)]
            for k in (2, 1, 3):
                send(spot, spot, ("g2", t), ("g2", t, k), device(**{STREAMS[s][1]: k}))
            for k in (1, 3):
                send(spot, spot, ("g3", t), ("g3", t, 0), device(**{STREAMS[s][2]: k}))

        if t == 0:
            arrived(res_recv, "res")
            hidden[other] = res_recv[...]
        arrived(z_sib.at[1], ("zs", t))
        rows = slice(r0, r0 + n)
        mine = hidden[c, rows] + z_own[c]
        theirs = hidden[other, rows] + unpack(z_sib[1])
        arrived(z_recv, ("z", t))
        for j in range(3):
            mine = mine + unpack(z_recv[j, c])
            theirs = theirs + unpack(z_recv[j, other])
        hidden[c, rows] = mine
        hidden[other, rows] = theirs
        sent = jnp.concatenate([hidden[0, rows], hidden[1, rows]], axis=0).astype(BF16)
        for s, (a1, a2, a3) in enumerate(STREAMS):
            p1, p2, p3 = place[s]
            x_all[c, s, p3, p2, p1] = sent[:, s * W : (s + 1) * W]
            for j in (2, 1, 3):
                spot = x_all.at[c, s, p3, p2, p1]
                send(spot, spot, ("g1", t), ("g1", t, j), device(**{a1: j}))
        for s in range(3):
            pass_on(s, 0)

        def row(s, j3, j2, core):
            _, p2, p3 = place[s]
            return x_all.at[core, s, wrap(p3 + j3), wrap(p2 + j2)]

        def share_key(j3, j2):
            if j3 == 0:
                return ("gs", t, 0, j2 == 0)
            if j3 == 2:
                return ("gs", t, 2, j2 == 2)
            return ("gs", t, 1, j2 in (0, 1))

        def share(s, j3, j2):
            spot = row(s, j3, j2, c)
            send(spot, spot, ("gs", t), share_key(j3, j2), sibling)

        def shared(j3, j2):
            key = share_key(j3, j2)
            if j3 == 1:
                arrived(x_all.at[other, :, 0], key)
            elif key[3]:
                arrived(x_all.at[other, :, 0, 0], key)
            else:
                arrived(x_all.at[other, :, 0, pl.ds(0, 3)], key)

        def take1():
            for j in (1, 3, 2):
                arrived(x_all.at[c, :, 0, 0, 0], ("g1", t, j))
                for s in range(3):
                    pass_on(s, j)
            for s in range(3):
                share(s, 0, 0)

        def take2(j):
            arrived(x_all.at[c, :, 0, 0], ("g2", t, j))
            for s in range(3):
                spot = row(s, 0, 4 - j, c)
                for k in (1, 3):
                    send(spot, spot, ("g3", t), ("g3", t, 4 - j), device(**{STREAMS[s][2]: k}))
                share(s, 0, 4 - j)

        def take3(j2):
            arrived(x_all.at[c, :, 0, pl.ds(0, 2)], ("g3", t, j2))
            for s in range(3):
                for j in (1, 3):
                    spot = row(s, -j, j2, c)
                    half = spot.at[pl.ds(0 if j == 1 else 2, 2)]
                    send(half, half, ("g3", t), ("g4", t, j2), device(**{STREAMS[s][2]: j}))
                    share(s, 4 - j, j2)

        def take4(j2):
            arrived(x_all.at[c, :, 0, 0], ("g4", t, j2))
            for s in range(3):
                share(s, 2, j2)

        def multiply(xs, k0, spots):
            g = u = sq = None
            for h in range(2):
                x = jnp.concatenate([v.reshape(4 * b, W) for v in xs[h]], axis=0).astype(F32)
                k = k0 + h
                part_sq = x * x
                part_sq = part_sq[:, :128] + part_sq[:, 128:]
                xb = (x * gain[k]).astype(BF16)
                weight_rows = pl.ds(pl.multiple_of(k * W, W), W)
                part_g = jnp.dot(xb, wg[weight_rows, :], preferred_element_type=F32)
                part_u = jnp.dot(xb, wu[weight_rows, :], preferred_element_type=F32)
                g = part_g if g is None else g + part_g
                u = part_u if u is None else u + part_u
                sq = part_sq if sq is None else sq + part_sq
            for i, spot in enumerate(spots):
                m4 = slice(i * 4 * b, (i + 1) * 4 * b)
                acc_g[spot] = acc_g[spot] + g[m4].reshape(4, b, W)
                acc_u[spot] = acc_u[spot] + u[m4].reshape(4, b, W)
                ssum[spot] = ssum[spot] + sq[m4].reshape(4, b, 128)

        def rows_01(j3s, j2s):
            qs = [[wrap(place[s][2] + j3) for j3 in j3s] for s in range(2)]
            rs = [[wrap(place[s][1] + j2) for j2 in j2s] for s in range(2)]
            for q in qs[0]:
                multiply([[x_all[h, 0, q, r] for r in rs[0]] for h in range(2)], q * 6, [(r,) for r in rs[0]])
            for r in rs[1]:
                xs = [[x_all[h, 1, q, r] for q in qs[1]] for h in range(2)]
                multiply(xs, r * 6 + 2, [(slice(None), q) for q in qs[1]])

        def planes_2(j3s):
            qs = [wrap(place[2][2] + j3) for j3 in j3s]
            for z in range(4):
                multiply([[x_all[h, 2, q, :, z] for q in qs] for h in range(2)], z * 6 + 4, [(q,) for q in qs])

        take1()
        if t == 0:
            for cp in w_copies:
                cp.wait()
        shared(0, 0)
        rows_01((0,), (0,))
        take2(1)
        take2(3)
        take2(2)
        take3(0)
        info_2()
        shared(0, 1)
        rows_01((0,), (1, 3))
        take3(1)
        rows_01((0,), (2,))
        planes_2((0,))
        take3(3)
        shared(1, 0)
        rows_01((1, 3), (0, 1))
        take3(2)
        take4(0)
        take4(1)
        info_3()
        shared(1, 3)
        rows_01((1, 3), (3, 2))
        take4(3)
        planes_2((1, 3))
        take4(2)
        shared(2, 0)
        rows_01((2,), (0, 1, 3))
        shared(2, 2)
        rows_01((2,), (2,))
        planes_2((2,))

        if t == 0:
            arrived(info.at[other], "ic")
        lane4 = lax.broadcasted_iota(jnp.int32, (4, b, 128), 2)

        def activate(i, carry):
            both = jnp.concatenate([info[0, i, :, rows], info[1, i, :, rows]], axis=1)
            chosen = jnp.sum(jnp.where(lane4 == me["x"], both, 0.0), axis=2, keepdims=True)
            inv = lax.rsqrt(jnp.sum(ssum[i], axis=2, keepdims=True) / D + 1e-05)
            g = acc_g[i] * inv
            u = acc_u[i] * inv
            act[c, i] = (g / (1.0 + jnp.exp(-g)) * u * chosen).astype(BF16)
            send(act.at[c, i], act.at[c, i], ("act", t), ("act", t), sibling)
            return carry

        lax.fori_loop(0, 4, activate, 0, unroll=2)
        if t == 0:
            local(wd.at[:, :, down_rows(0)], wd.at[:, :, down_rows(0)], 6).wait()
            arrived(wd.at[:, :, down_rows(0)], "wd")
        arrived(act.at[other], ("act", t))

        def down(s, j3):
            q = wrap(place[s][2] + j3)

            def step(i, carry):
                pick = (i,) if s == 0 else ((slice(None), q) if s == 1 else (q,))
                a = jnp.concatenate([act[(h,) + pick].reshape(4 * b, W) for h in range(2)], axis=1)
                w = wd[q if s == 0 else i, s]
                y = jnp.dot(a, w, preferred_element_type=F32).reshape(4, b, W).astype(BF16)
                if s == 2:
                    part[s, j3, :, i] = y
                else:
                    part[s, j3, i] = y
                return carry

            lax.fori_loop(0, 4, step, 0, unroll=4)

        def second(s, j2):
            return wrap(place[s][1] + j2)

        def send_far(s):
            for j2 in (2, 3, 1, 0):
                j = 1 if j2 in FORWARD_UP else 3
                r = second(s, j2)
                send(part.at[s, 2, r], d2_in.at[s, r], ("r4", t), ("r4", t, j2), device(**{STREAMS[s][2]: j}))

        def send_near(s, j, j2):
            r = second(s, j2)
            to = device(**{STREAMS[s][2]: j})
            send(part.at[s, j, r], plane_in.at[s, j // 2, r], ("r3", t), ("r3", t, j2), to)

        def add_far(j2):
            j = 1 if j2 in FORWARD_UP else 3
            arrived(d2_in.at[:, 0], ("r4", t, j2))
            for s in range(3):
                r = second(s, j2)
                part[s, j, r] = (part[s, j, r].astype(F32) + d2_in[s, r].astype(F32)).astype(BF16)
                send_near(s, j, j2)

        for s in range(3):
            down(s, 2)
            send_far(s)
        for s in range(3):
            down(s, 1)
            send_near(s, 1, 2)
            down(s, 3)
            send_near(s, 3, 3)
        for s in range(3):
            down(s, 0)
        add_far(2)
        add_far(3)
        for s in range(3):
            send_near(s, 1, 1)
        add_far(1)
        add_far(0)
        for s in range(3):
            send_near(s, 3, 0)
        for j2 in (2, 3, 1, 0):
            arrived(plane_in.at[:, :, 0], ("r3", t, j2))
            for s in range(3):
                r = second(s, j2)
                v = part[s, 0, r].astype(F32) + plane_in[s, 0, r].astype(F32) + plane_in[s, 1, r].astype(F32)
                if j2:
                    row_out[s, j2 - 1] = v.astype(BF16)
                    to = device(**{STREAMS[s][1]: j2})
                    send(row_out.at[s, j2 - 1], row_in.at[s, j2 - 1], ("r2", t), ("r2", t, s), to)
                else:
                    row_own[s] = v
        for s in range(3):
            arrived(row_in.at[s], ("r2", t, s))
            row_own[s] = row_own[s] + (
                row_in[s, 0].astype(F32) + row_in[s, 1].astype(F32) + row_in[s, 2].astype(F32)
            )
            for j1 in (2, 1, 3):
                blk_out[s, j1 - 1] = row_own[s, wrap(place[s][0] + j1)].astype(BF16)
                to = device(**{STREAMS[s][0]: j1})
                send(blk_out.at[s, j1 - 1], blk_in.at[s, j1 - 1], ("r1", t), ("r1", t, s), to)
        drain(z_send, ("z", t))
        drain(z_sib.at[0], ("zs", t))
        drain(x_all.at[c, :, 0, 0, pl.ds(0, 3)], ("g1", t))
        drain(x_all.at[c, :, 0, pl.ds(0, 3)], ("g2", t))
        drain(x_all.at[c, :, pl.ds(0, 3)], ("g3", t))
        drain(x_all.at[c], ("gs", t))
        drain(act.at[c], ("act", t))
        drain(d2_in, ("r4", t))
        drain(plane_in, ("r3", t))
        drain(row_out, ("r2", t))
        for s in range(3):
            v = row_own[s, place[s][0]]
            arrived(blk_in.at[s], ("r1", t, s))
            for j in range(3):
                v = v + blk_in[s, j].astype(F32)
            for k in range(2):
                fin_send[k, s] = hidden[k, rows, s * W : (s + 1) * W] + v[k * n : (k + 1) * n]
            send(fin_send.at[other, s], fin.at[s], ("fin", t), ("fin", t), sibling)
        drain(blk_out, ("r1", t))
        arrived(fin, ("fin", t))
        drain(fin, ("fin", t))
        for s in range(3):
            fin_send[other, s] = fin[s]
            for h in range(2):
                result[rows, s * 512 + h * W : s * 512 + (h + 1) * W] = fin_send[h, s]

    flow(0)
    drain(res_send, "res")
    drain(info.at[c, 0, pl.ds(0, 3)], "ix")
    drain(info.at[c, pl.ds(0, 3)], "iy")
    drain(info.at[c], "ic")
    drain(wd.at[:, :, down_rows(0)], "wd")
    out[...] = result[...].astype(BF16)


def local_step(
    new_query, new_kv, kv_cache, lengths, residual, out_proj, expert_ids, gate_weights, slot_expert, moe_gain,
    w_gate, w_up, w_down,
):
    vmem = pl.BlockSpec(memory_space=pltpu.VMEM)
    smem = pl.BlockSpec(memory_space=pltpu.SMEM)
    anywhere = pl.BlockSpec(memory_space=pl.ANY)
    scratch = list(common_scratch().values())
    for _, n in PARTS:
        scratch += list(part_scratch(n).values())
    return pl.pallas_call(
        kernel,
        out_shape=jax.ShapeDtypeStruct((R, QD), BF16),
        in_specs=[smem, smem] + [vmem] * 6 + [anywhere] * 5,
        out_specs=vmem,
        scratch_shapes=scratch,
        compiler_params=pltpu.CompilerParams(
            collective_id=0, has_side_effects=True, vmem_limit_bytes=62 * 2**20
        ),
        name="decode_layer",
    )(
        lengths, slot_expert, new_query, new_kv, residual, expert_ids.T, gate_weights.T,
        moe_gain.reshape(D // W, 1, W), kv_cache, out_proj, w_gate, w_up, w_down,
    )


def solution(mesh):
    placed = (
        P(("attn", "exp"), "tp"),
        P(("attn", "exp"), None, "tp"),
        P(("attn", "exp"), None, None, "tp"),
        P(("attn", "exp")),
        P(("attn", "exp"), None),
        P("tp", None),
        P(("attn", "exp"), None),
        P(("attn", "exp"), None),
        P(),
        P(),
        P("exp", None, ("attn", "tp")),
        P("exp", None, ("attn", "tp")),
        P("exp", ("attn", "tp"), None),
    )
    return jax.shard_map(
        local_step, mesh=mesh, in_specs=placed, out_specs=P(("attn", "exp"), "tp"), check_vma=False
    )
```

```python
import jax
import jax.numpy as jnp
from jax import lax
from jax.experimental import pallas as pl
from jax.experimental.pallas import tpu as pltpu
from jax.sharding import PartitionSpec as P

MESH = pl.DeviceIdType.MESH
F32 = jnp.float32
BF16 = jnp.bfloat16

HD = 128
HEADS = 6
R = 24
CACHE = 512
D = 6144
QD = 1536
W = 256
SEMS = 44
SENDS = 20
PARTS = ((0, R),)
CHUNK = 6

STREAMS = (("x", "y", "z"), ("y", "z", "x"), ("z", "x", "y"))
FORWARD_UP = (0, 3)
FORWARD_DOWN = (1, 2)


def wrap(v):
    return lax.rem(v + 4, 4)


def common_scratch():
    v = pltpu.VMEM
    return dict(
        k_buf=v((R, CACHE, HD), BF16),
        v_buf=v((R, CACHE, HD), BF16),
        op_buf=v((4, HEADS * HD, QD), BF16),
        wg=v((D, W), BF16),
        wu=v((D, W), BF16),
        wd=v((4, 3, 2 * W, W), BF16),
        q_pad=v((R * 8, HD), F32),
        kn=v((R * 8, HD), F32),
        vn=v((R * 8, HD), F32),
        scores=v((R * 8, CACHE), F32),
        attn_out=v((R * 8, HD), F32),
        info_pad=v((128, 128), F32),
        info=v((2, 4, 4, R, 128), F32),
        res_send=v((R, 3 * W), F32),
        res_recv=v((R, 3 * W), F32),
        hidden=v((2, R, 3 * W), F32),
        hidden_in=v((R, 3 * W), F32),
        result=v((R, QD), F32),
        send_sems=pltpu.SemaphoreType.DMA((SENDS,)),
        recv_sems=pltpu.SemaphoreType.DMA((SEMS,)),
        local_sems=pltpu.SemaphoreType.DMA((7 + 2 * (R // CHUNK),)),
    )


def part_scratch(n):
    v, b = pltpu.VMEM, 2 * n
    return dict(
        z_send=v((3, 2, b, 384), BF16),
        z_recv=v((3, 2, b, 384), BF16),
        z_sib=v((2, b, 384), BF16),
        z_own=v((2, n, 3 * W), F32),
        x_all=v((2, 3, 4, 4, 4, b, W), BF16),
        ssum=v((4, 4, b, 128), F32),
        acc_g=v((4, 4, b, W), F32),
        acc_u=v((4, 4, b, W), F32),
        act=v((2, 4, 4, b, W), BF16),
        part=v((3, 4, 4, 4, b, W), BF16),
        d2_in=v((3, 4, 4, b, W), BF16),
        plane_in=v((3, 2, 4, 4, b, W), BF16),
        row_out=v((3, 3, 4, b, W), BF16),
        row_in=v((3, 3, 4, b, W), BF16),
        row_own=v((3, 4, b, W), F32),
        blk_out=v((3, 3, 2, b, 128), BF16),
        blk_in=v((3, 3, 2, b, 128), BF16),
        fin_send=v((2, 3, n, W), F32),
        fin=v((3, n, W), F32),
    )


def kernel(*refs):
    (lengths, slot_expert, query, new_kv, residual, ids, gate_w, gain, cache, out_proj, w_gate, w_up, w_down, out) = refs[:14]
    names = common_scratch()
    m = dict(zip(names, refs[14:]))
    at = 14 + len(names)
    buffers = []
    for _, n in PARTS:
        names = part_scratch(n)
        buffers.append(dict(zip(names, refs[at:])))
        at += len(names)
    k_buf, v_buf, op_buf, wg, wu, wd = (m[k] for k in ("k_buf", "v_buf", "op_buf", "wg", "wu", "wd"))
    q_pad, kn, vn, scores, attn_out = (m[k] for k in ("q_pad", "kn", "vn", "scores", "attn_out"))
    info, res_send, res_recv, hidden, result = (m[k] for k in ("info", "res_send", "res_recv", "hidden", "result"))
    hidden_in = m["hidden_in"]
    info_pad, send_sems, recv_sems, local_sems = (m[k] for k in ("info_pad", "send_sems", "recv_sems", "local_sems"))

    attn = lax.axis_index("attn")
    me = {"y": attn // 2, "c": lax.rem(attn, 2), "z": lax.axis_index("tp"), "x": lax.axis_index("exp")}
    c, other = me["c"], 1 - me["c"]
    place = [tuple(me[a] for a in axes) for axes in STREAMS]

    def device(c=None, **steps):
        at = dict(me)
        for axis, step in steps.items():
            at[axis] = wrap(at[axis] + step)
        if c is not None:
            at["c"] = c
        return (at["y"] * 2 + at["c"], at["z"], at["x"])

    sibling = device(c=other)

    def local(src, dst, i):
        return pltpu.make_async_copy(src, dst, local_sems.at[i])

    op_copies = {
        j: local(out_proj.at[:, pl.ds(pl.multiple_of(wrap(me["z"] + j) * QD, QD), QD)], op_buf.at[j], j)
        for j in (2, 1, 3, 0)
    }
    w_copies = [local(w_gate.at[0], wg, 4), local(w_up.at[0], wu, 5)]
    k_copies, v_copies = [], []
    for i in range(R // CHUNK):
        some = pl.ds(i * CHUNK, CHUNK)
        k_copies.append(local(cache.at[some, 0], k_buf.at[some], 7 + 2 * i))
        v_copies.append(local(cache.at[some, 1], v_buf.at[some], 8 + 2 * i))

    def down_columns(z, s, h):
        return w_down.at[0, :, pl.ds(pl.multiple_of(z * QD + s * 512 + h * W, W), W)]

    def down_rows(core):
        return pl.ds(pl.multiple_of(core * W, W), W)

    for cp in k_copies + v_copies:
        cp.start()
    for j in (2, 1, 3, 0):
        op_copies[j].start()

    barrier = pltpu.get_barrier_semaphore()
    partners = [device(c=k, z=j) for j in (1, 2, 3) for k in (0, 1)] + [sibling]
    partners += [device(c=k, **{a: j}) for a in ("x", "y") for j in (1, 2, 3) for k in (0, 1)]
    for p in partners:
        pl.semaphore_signal(barrier, inc=1, device_id=p, device_id_type=MESH)

    table, classes = {}, {}

    def sem(key):
        if key not in table:
            table[key] = len(table)
            assert len(table) <= SEMS
        return recv_sems.at[table[key]]

    def left(kind):
        if kind not in classes:
            classes[kind] = len(classes)
            assert len(classes) <= SENDS
        return send_sems.at[classes[kind]]

    def send(src, dst, kind, key, to):
        pltpu.make_async_remote_copy(
            src_ref=src, dst_ref=dst, send_sem=left(kind), recv_sem=sem(key), device_id=to, device_id_type=MESH
        ).start()

    def arrived(dst, key):
        pltpu.make_async_remote_copy(
            src_ref=dst, dst_ref=dst, send_sem=send_sems.at[0], recv_sem=sem(key),
            device_id=sibling, device_id_type=MESH,
        ).wait_recv()

    def drain(src, kind):
        pltpu.make_async_remote_copy(
            src_ref=src, dst_ref=src, send_sem=left(kind), recv_sem=recv_sems.at[0],
            device_id=sibling, device_id_type=MESH,
        ).wait_send()

    info_pad[...] = jnp.zeros_like(info_pad)
    for s in range(4):
        hit = jnp.where(ids[...] == slot_expert[s], gate_w[...], 0.0)
        info_pad[s : s + 1, :R] = jnp.sum(hit, axis=0, keepdims=True)
    info[c, me["y"], me["x"]] = info_pad[...].T[:R]

    def res_part(h):
        return jnp.concatenate(
            [residual[:, pl.ds(pl.multiple_of(me["z"] * QD + s * 512 + h * W, W), W)] for s in range(3)], axis=1
        ).astype(F32)

    res_send[...] = res_part(other)
    hidden[c] = res_part(c)
    for h in range(8):
        if h < HEADS:
            q_pad[pl.ds(h, R, stride=8), :] = query[:, h * HD : (h + 1) * HD].astype(F32)
        else:
            q_pad[pl.ds(h, R, stride=8), :] = jnp.zeros((R, HD), F32)
        kn[pl.ds(h, R, stride=8), :] = new_kv[:, 0, :].astype(F32)
        vn[pl.ds(h, R, stride=8), :] = new_kv[:, 1, :].astype(F32)

    def begin_links():
        pl.semaphore_wait(barrier, len(partners))
        send(res_send, res_recv, "res", "res", sibling)

    def info_1():
        for j in (1, 3, 2):
            spot = info.at[c, me["y"], me["x"]]
            send(spot, spot, "ix", "ix", device(x=j))

    def info_2():
        arrived(info.at[c, 0, pl.ds(0, 3)], "ix")
        for j in (1, 3, 2):
            spot = info.at[c, me["y"]]
            send(spot, spot, "iy", "iy", device(y=j))

    def info_3():
        arrived(info.at[c, pl.ds(0, 3)], "iy")
        send(info.at[c], info.at[c], "ic", "ic", sibling)

    def load_weights():
        for cp in w_copies:
            cp.start()
        for z in range(4):
            for s in range(3):
                send(down_columns(z, s, other), wd.at[z, s, down_rows(c)], "wd", "wd", sibling)
                local(down_columns(z, s, c), wd.at[z, s, down_rows(c)], 6).start()

    def pack(v):
        return jnp.concatenate([v[:, :384], v[:, 384:]], axis=0).astype(BF16)

    def flow(t):
        r0, n = PARTS[t]
        b = 2 * n
        p = buffers[t]
        z_send, z_recv, z_sib, z_own = (p[k] for k in ("z_send", "z_recv", "z_sib", "z_own"))
        x_all, ssum, acc_g, acc_u, act = (p[k] for k in ("x_all", "ssum", "acc_g", "acc_u", "act"))
        part, d2_in, plane_in = (p[k] for k in ("part", "d2_in", "plane_in"))
        row_out, row_in, row_own, blk_out, blk_in = (p[k] for k in ("row_out", "row_in", "row_own", "blk_out", "blk_in"))
        fin_send, fin = p["fin_send"], p["fin"]

        scale = HD ** (-0.5)
        position = lax.broadcasted_iota(jnp.int32, (8, CACHE), 1)
        mine8 = slice(r0 * 8, (r0 + n) * 8)
        for r in range(r0, r0 + n):
            if r % CHUNK == 0:
                k_copies[r // CHUNK].wait()
            s = lax.dot_general(
                q_pad[r * 8 : r * 8 + 8, :].astype(BF16), k_buf[r], (((1,), (1,)), ((), ())),
                preferred_element_type=F32,
            ) * scale
            scores[r * 8 : r * 8 + 8, :] = jnp.where(position < lengths[r], s, -1e30)
        own_score = jnp.sum(q_pad[mine8, :] * kn[mine8, :], axis=1, keepdims=True) * scale
        raw = scores[mine8, :]
        top = jnp.maximum(jnp.max(raw, axis=1, keepdims=True), own_score)
        weight = jnp.exp(raw - top)
        own_weight = jnp.exp(own_score - top)
        total = jnp.sum(weight, axis=1, keepdims=True) + own_weight
        scores[mine8, :] = weight / total
        own_prob = (own_weight / total).astype(BF16).astype(F32)
        for r in range(r0, r0 + n):
            if r % CHUNK == 0:
                v_copies[r // CHUNK].wait()
            attn_out[r * 8 : r * 8 + 8, :] = jnp.dot(
                scores[r * 8 : r * 8 + 8, :].astype(BF16), v_buf[r], preferred_element_type=F32
            )
        attn_out[mine8, :] = attn_out[mine8, :] + own_prob * vn[mine8, :]
        attended = jnp.concatenate(
            [attn_out[pl.ds(r0 * 8 + h, n, stride=8), :] for h in range(HEADS)], axis=1
        ).astype(BF16)

        def unpack(v):
            v = v.astype(F32)
            return jnp.concatenate([v[:n], v[n:]], axis=1)

        for j in (2, 1, 3, 0):
            if t == 0:
                op_copies[j].wait()
            term = jnp.dot(attended, op_buf[j], preferred_element_type=F32)
            halves = [
                jnp.concatenate([term[:, s * 512 + h * W : s * 512 + (h + 1) * W] for s in range(3)], axis=1)
                for h in range(2)
            ]
            if j == 2 and t == 0:
                begin_links()
            if j:
                for h in range(2):
                    z_send[j - 1, h] = pack(halves[h])
                    send(z_send.at[j - 1, h], z_recv.at[j - 1, c], ("z", t), ("z", t), device(c=h, z=j))
            else:
                z_own[0] = halves[0]
                z_own[1] = halves[1]
                z_sib[0] = pack(z_own[other])
                send(z_sib.at[0], z_sib.at[1], ("zs", t), ("zs", t), sibling)
        info_1()
        load_weights()
        acc_g[...] = jnp.zeros_like(acc_g)
        acc_u[...] = jnp.zeros_like(acc_u)
        ssum[...] = jnp.zeros_like(ssum)

        def pass_on(s, j):
            p1, p2, p3 = place[s]
            spot = x_all.at[c, s, p3, p2, wrap(p1 - j)]
            for k in (1, 3, 2):
                send(spot, spot, ("g2", t), ("g2", t, k), device(**{STREAMS[s][1]: k}))
            for k in (1, 3):
                send(spot, spot, ("g3", t), ("g3", t, 0), device(**{STREAMS[s][2]: k}))

        if t == 0:
            arrived(res_recv, "res")
            hidden[other] = res_recv[...]
        arrived(z_sib.at[1], ("zs", t))
        rows = slice(r0, r0 + n)
        mine = hidden[c, rows] + z_own[c]
        theirs = hidden[other, rows] + unpack(z_sib[1])
        arrived(z_recv, ("z", t))
        for j in range(3):
            mine = mine + unpack(z_recv[j, c])
            theirs = theirs + unpack(z_recv[j, other])
        hidden[c, rows] = mine
        hidden[other, rows] = theirs
        sent = jnp.concatenate([hidden[0, rows], hidden[1, rows]], axis=0).astype(BF16)
        for s, (a1, a2, a3) in enumerate(STREAMS):
            p1, p2, p3 = place[s]
            x_all[c, s, p3, p2, p1] = sent[:, s * W : (s + 1) * W]
            for j in (2, 1, 3):
                spot = x_all.at[c, s, p3, p2, p1]
                send(spot, spot, ("g1", t), ("g1", t, j), device(**{a1: j}))
        for s in range(3):
            pass_on(s, 0)
        send(hidden.at[other], hidden_in, "hid", "hid", sibling)

        def row(s, j3, j2, core):
            _, p2, p3 = place[s]
            return x_all.at[core, s, wrap(p3 + j3), wrap(p2 + j2)]

        def share_key(j3, j2):
            if j3 == 0:
                return ("gs", t, 0, j2 == 0)
            if j3 == 2:
                return ("gs", t, 2, j2 == 2)
            return ("gs", t, 1, j2 in (0, 1))

        def share(s, j3, j2):
            spot = row(s, j3, j2, c)
            send(spot, spot, ("gs", t), share_key(j3, j2), sibling)

        def shared(j3, j2):
            key = share_key(j3, j2)
            if j3 == 1:
                arrived(x_all.at[other, :, 0], key)
            elif key[3]:
                arrived(x_all.at[other, :, 0, 0], key)
            else:
                arrived(x_all.at[other, :, 0, pl.ds(0, 3)], key)

        def take1():
            for j in (1, 3, 2):
                arrived(x_all.at[c, :, 0, 0, 0], ("g1", t, j))
                for s in range(3):
                    pass_on(s, j)
            for s in range(3):
                share(s, 0, 0)

        def take2(j):
            arrived(x_all.at[c, :, 0, 0], ("g2", t, j))
            for s in range(3):
                spot = row(s, 0, 4 - j, c)
                for k in (1, 3):
                    send(spot, spot, ("g3", t), ("g3", t, 4 - j), device(**{STREAMS[s][2]: k}))
                share(s, 0, 4 - j)

        def take3(j2):
            arrived(x_all.at[c, :, 0, pl.ds(0, 2)], ("g3", t, j2))
            for s in range(3):
                for j in (1, 3):
                    spot = row(s, -j, j2, c)
                    half = spot.at[pl.ds(0 if j == 1 else 2, 2)]
                    send(half, half, ("g3", t), ("g4", t, j2), device(**{STREAMS[s][2]: j}))
                    share(s, 4 - j, j2)

        def take4(j2):
            arrived(x_all.at[c, :, 0, 0], ("g4", t, j2))
            for s in range(3):
                share(s, 2, j2)

        def multiply(xs, k0, spots):
            g = u = sq = None
            for h in range(2):
                x = jnp.concatenate([v.reshape(4 * b, W) for v in xs[h]], axis=0).astype(F32)
                k = k0 + h
                part_sq = x * x
                part_sq = part_sq[:, :128] + part_sq[:, 128:]
                xb = (x * gain[k]).astype(BF16)
                weight_rows = pl.ds(pl.multiple_of(k * W, W), W)
                part_g = jnp.dot(xb, wg[weight_rows, :], preferred_element_type=F32)
                part_u = jnp.dot(xb, wu[weight_rows, :], preferred_element_type=F32)
                g = part_g if g is None else g + part_g
                u = part_u if u is None else u + part_u
                sq = part_sq if sq is None else sq + part_sq
            for i, spot in enumerate(spots):
                m4 = slice(i * 4 * b, (i + 1) * 4 * b)
                acc_g[spot] = acc_g[spot] + g[m4].reshape(4, b, W)
                acc_u[spot] = acc_u[spot] + u[m4].reshape(4, b, W)
                ssum[spot] = ssum[spot] + sq[m4].reshape(4, b, 128)

        def rows_01(j3s, j2s):
            qs = [[wrap(place[s][2] + j3) for j3 in j3s] for s in range(2)]
            rs = [[wrap(place[s][1] + j2) for j2 in j2s] for s in range(2)]
            for q in qs[0]:
                multiply([[x_all[h, 0, q, r] for r in rs[0]] for h in range(2)], q * 6, [(r,) for r in rs[0]])
            for r in rs[1]:
                xs = [[x_all[h, 1, q, r] for q in qs[1]] for h in range(2)]
                multiply(xs, r * 6 + 2, [(slice(None), q) for q in qs[1]])

        def planes_2(j3s):
            qs = [wrap(place[2][2] + j3) for j3 in j3s]
            for z in range(4):
                multiply([[x_all[h, 2, q, :, z] for q in qs] for h in range(2)], z * 6 + 4, [(q,) for q in qs])

        take1()
        if t == 0:
            for cp in w_copies:
                cp.wait()
        shared(0, 0)
        rows_01((0,), (0,))
        take2(1)
        take2(3)
        take2(2)
        take3(0)
        info_2()
        shared(0, 1)
        rows_01((0,), (1, 3))
        take3(1)
        rows_01((0,), (2,))
        planes_2((0,))
        take3(3)
        shared(1, 0)
        rows_01((1, 3), (0, 1))
        take3(2)
        take4(0)
        take4(1)
        info_3()
        shared(1, 3)
        rows_01((1, 3), (3, 2))
        take4(3)
        planes_2((1, 3))
        take4(2)
        shared(2, 0)
        rows_01((2,), (0, 1, 3))
        shared(2, 2)
        rows_01((2,), (2,))
        planes_2((2,))

        if t == 0:
            arrived(info.at[other], "ic")
        lane4 = lax.broadcasted_iota(jnp.int32, (4, b, 128), 2)

        def activate(i, carry):
            both = jnp.concatenate([info[0, i, :, rows], info[1, i, :, rows]], axis=1)
            chosen = jnp.sum(jnp.where(lane4 == me["x"], both, 0.0), axis=2, keepdims=True)
            inv = lax.rsqrt(jnp.sum(ssum[i], axis=2, keepdims=True) / D + 1e-05)
            g = acc_g[i] * inv
            u = acc_u[i] * inv
            act[c, i] = (g / (1.0 + jnp.exp(-g)) * u * chosen).astype(BF16)
            send(act.at[c, i], act.at[c, i], ("act", t), ("act", t), sibling)
            return carry

        lax.fori_loop(0, 4, activate, 0, unroll=2)
        if t == 0:
            local(wd.at[:, :, down_rows(0)], wd.at[:, :, down_rows(0)], 6).wait()
            arrived(wd.at[:, :, down_rows(0)], "wd")
        arrived(act.at[other], ("act", t))

        def down(s, j3):
            q = wrap(place[s][2] + j3)

            def step(i, carry):
                pick = (i,) if s == 0 else ((slice(None), q) if s == 1 else (q,))
                a = jnp.concatenate([act[(h,) + pick].reshape(4 * b, W) for h in range(2)], axis=1)
                w = wd[q if s == 0 else i, s]
                y = jnp.dot(a, w, preferred_element_type=F32).reshape(4, b, W).astype(BF16)
                if s == 2:
                    part[s, j3, :, i] = y
                else:
                    part[s, j3, i] = y
                return carry

            lax.fori_loop(0, 4, step, 0, unroll=4)

        def second(s, j2):
            return wrap(place[s][1] + j2)

        def send_far(s):
            for j2 in (2, 3, 1, 0):
                j = 1 if j2 in FORWARD_UP else 3
                r = second(s, j2)
                send(part.at[s, 2, r], d2_in.at[s, r], ("r4", t), ("r4", t, j2), device(**{STREAMS[s][2]: j}))

        def send_near(s, j, j2):
            r = second(s, j2)
            to = device(**{STREAMS[s][2]: j})
            send(part.at[s, j, r], plane_in.at[s, j // 2, r], ("r3", t), ("r3", t, j2), to)

        def add_far(j2):
            j = 1 if j2 in FORWARD_UP else 3
            arrived(d2_in.at[:, 0], ("r4", t, j2))
            for s in range(3):
                r = second(s, j2)
                part[s, j, r] = (part[s, j, r].astype(F32) + d2_in[s, r].astype(F32)).astype(BF16)
                send_near(s, j, j2)

        for s in range(3):
            down(s, 2)
            send_far(s)
        for s in range(3):
            down(s, 1)
            send_near(s, 1, 2)
            down(s, 3)
            send_near(s, 3, 3)
        for s in range(3):
            down(s, 0)
        add_far(2)
        add_far(3)
        for s in range(3):
            send_near(s, 1, 1)
        add_far(1)
        add_far(0)
        for s in range(3):
            send_near(s, 3, 0)
        for j2 in (2, 3, 1, 0):
            arrived(plane_in.at[:, :, 0], ("r3", t, j2))
            for s in range(3):
                r = second(s, j2)
                v = part[s, 0, r].astype(F32) + plane_in[s, 0, r].astype(F32) + plane_in[s, 1, r].astype(F32)
                if j2:
                    row_out[s, j2 - 1] = v.astype(BF16)
                    to = device(**{STREAMS[s][1]: j2})
                    send(row_out.at[s, j2 - 1], row_in.at[s, j2 - 1], ("r2", t), ("r2", t, s), to)
                else:
                    row_own[s] = v
        def fold(v):
            return jnp.concatenate([v[:, :128], v[:, 128:]], axis=0).astype(BF16)

        def unfold(v):
            v = v.astype(F32)
            return jnp.concatenate([v[:n], v[n:]], axis=1)

        for s in range(3):
            arrived(row_in.at[s], ("r2", t, s))
            row_own[s] = row_own[s] + (
                row_in[s, 0].astype(F32) + row_in[s, 1].astype(F32) + row_in[s, 2].astype(F32)
            )
            for j1 in (2, 1, 3):
                v = row_own[s, wrap(place[s][0] + j1)]
                for k in range(2):
                    blk_out[s, j1 - 1, k] = fold(v[k * n : (k + 1) * n])
                    to = device(c=k, **{STREAMS[s][0]: j1})
                    send(blk_out.at[s, j1 - 1, k], blk_in.at[s, j1 - 1, c], ("r1", t), ("r1", t, s), to)
            v = row_own[s, place[s][0]]
            for k in range(2):
                fin_send[k, s] = v[k * n : (k + 1) * n]
            send(fin_send.at[other, s], fin.at[s], ("fin", t), ("fin", t), sibling)
        drain(z_send, ("z", t))
        drain(z_sib.at[0], ("zs", t))
        drain(x_all.at[c, :, 0, 0, pl.ds(0, 3)], ("g1", t))
        drain(x_all.at[c, :, 0, pl.ds(0, 3)], ("g2", t))
        drain(x_all.at[c, :, pl.ds(0, 3)], ("g3", t))
        drain(x_all.at[c], ("gs", t))
        drain(act.at[c], ("act", t))
        drain(d2_in, ("r4", t))
        drain(plane_in, ("r3", t))
        drain(row_out, ("r2", t))
        drain(hidden_in, "hid")
        arrived(hidden_in, "hid")
        arrived(fin, ("fin", t))
        drain(fin, ("fin", t))
        for s in range(3):
            cols = slice(s * W, (s + 1) * W)
            mine = hidden[c, :, cols] + fin_send[c, s]
            theirs = hidden_in[:, cols] + fin[s]
            arrived(blk_in.at[s], ("r1", t, s))
            for j in range(3):
                mine = mine + unfold(blk_in[s, j, c])
                theirs = theirs + unfold(blk_in[s, j, other])
            fin_send[c, s] = mine
            fin_send[other, s] = theirs
            for h in range(2):
                result[rows, s * 512 + h * W : s * 512 + (h + 1) * W] = fin_send[h, s]
        drain(blk_out, ("r1", t))

    flow(0)
    drain(res_send, "res")
    drain(info.at[c, 0, pl.ds(0, 3)], "ix")
    drain(info.at[c, pl.ds(0, 3)], "iy")
    drain(info.at[c], "ic")
    drain(wd.at[:, :, down_rows(0)], "wd")
    out[...] = result[...].astype(BF16)


def local_step(
    new_query, new_kv, kv_cache, lengths, residual, out_proj, expert_ids, gate_weights, slot_expert, moe_gain,
    w_gate, w_up, w_down,
):
    vmem = pl.BlockSpec(memory_space=pltpu.VMEM)
    smem = pl.BlockSpec(memory_space=pltpu.SMEM)
    anywhere = pl.BlockSpec(memory_space=pl.ANY)
    scratch = list(common_scratch().values())
    for _, n in PARTS:
        scratch += list(part_scratch(n).values())
    return pl.pallas_call(
        kernel,
        out_shape=jax.ShapeDtypeStruct((R, QD), BF16),
        in_specs=[smem, smem] + [vmem] * 6 + [anywhere] * 5,
        out_specs=vmem,
        scratch_shapes=scratch,
        compiler_params=pltpu.CompilerParams(
            collective_id=0, has_side_effects=True, vmem_limit_bytes=62 * 2**20
        ),
        name="decode_layer",
    )(
        lengths, slot_expert, new_query, new_kv, residual, expert_ids.T, gate_weights.T,
        moe_gain.reshape(D // W, 1, W), kv_cache, out_proj, w_gate, w_up, w_down,
    )


def solution(mesh):
    placed = (
        P(("attn", "exp"), "tp"),
        P(("attn", "exp"), None, "tp"),
        P(("attn", "exp"), None, None, "tp"),
        P(("attn", "exp")),
        P(("attn", "exp"), None),
        P("tp", None),
        P(("attn", "exp"), None),
        P(("attn", "exp"), None),
        P(),
        P(),
        P("exp", None, ("attn", "tp")),
        P("exp", None, ("attn", "tp")),
        P("exp", ("attn", "tp"), None),
    )
    return jax.shard_map(
        local_step, mesh=mesh, in_specs=placed, out_specs=P(("attn", "exp"), "tp"), check_vma=False
    )
```

```python
import jax
import jax.numpy as jnp
from jax import lax
from jax.experimental import pallas as pl
from jax.experimental.pallas import tpu as pltpu
from jax.sharding import PartitionSpec as P

MESH = pl.DeviceIdType.MESH
F32 = jnp.float32
BF16 = jnp.bfloat16

HD = 128
HEADS = 6
R = 24
CACHE = 512
D = 6144
QD = 1536
W = 256
SEMS = 46
SENDS = 20
PARTS = ((0, R),)
CHUNK = 6

STREAMS = (("x", "y", "z"), ("y", "z", "x"), ("z", "x", "y"))
FORWARD_UP = (0, 3)
FORWARD_DOWN = (1, 2)


def wrap(v):
    return lax.rem(v + 4, 4)


def common_scratch():
    v = pltpu.VMEM
    return dict(
        k_buf=v((R, CACHE, HD), BF16),
        v_buf=v((R, CACHE, HD), BF16),
        op_buf=v((4, HEADS * HD, QD), BF16),
        wg=v((D, W), BF16),
        wu=v((D, W), BF16),
        wd=v((4, 3, 2 * W, W), BF16),
        q_pad=v((R * 8, HD), F32),
        kn=v((R * 8, HD), F32),
        vn=v((R * 8, HD), F32),
        scores=v((R * 8, CACHE), F32),
        attn_out=v((R * 8, HD), F32),
        info_pad=v((128, 128), F32),
        info=v((2, 4, 4, R, 128), F32),
        res_send=v((R, 3 * W), F32),
        res_recv=v((R, 3 * W), F32),
        hidden=v((2, R, 3 * W), F32),
        hidden_in=v((R, 3 * W), F32),
        result=v((R, QD), F32),
        send_sems=pltpu.SemaphoreType.DMA((SENDS,)),
        recv_sems=pltpu.SemaphoreType.DMA((SEMS,)),
        local_sems=pltpu.SemaphoreType.DMA((7 + 2 * (R // CHUNK),)),
    )


def part_scratch(n):
    v, b = pltpu.VMEM, 2 * n
    return dict(
        z_send=v((3, 2, b, 384), BF16),
        z_recv=v((3, 2, b, 384), BF16),
        z_sib=v((2, b, 384), BF16),
        z_own=v((2, n, 3 * W), F32),
        x_all=v((2, 3, 4, 4, 4, b, W), BF16),
        ssum=v((4, 4, b, 128), F32),
        acc_g=v((4, 4, b, W), F32),
        acc_u=v((4, 4, b, W), F32),
        act=v((2, 4, 4, b, W), BF16),
        part=v((3, 4, 4, 4, b, W), BF16),
        d2_in=v((3, 4, 4, b, W), BF16),
        plane_in=v((3, 2, 4, 4, b, W), BF16),
        row_out=v((3, 3, 4, b, W), BF16),
        row_in=v((3, 3, 4, b, W), BF16),
        row_own=v((3, 4, b, W), F32),
        blk_out=v((3, 3, 2, b, 128), BF16),
        blk_in=v((3, 3, 2, b, 128), BF16),
        fin_send=v((2, 3, n, W), F32),
        fin=v((3, n, W), F32),
    )


def kernel(*refs):
    (lengths, slot_expert, query, new_kv, residual, ids, gate_w, gain, cache, out_proj, w_gate, w_up, w_down, out) = refs[:14]
    names = common_scratch()
    m = dict(zip(names, refs[14:]))
    at = 14 + len(names)
    buffers = []
    for _, n in PARTS:
        names = part_scratch(n)
        buffers.append(dict(zip(names, refs[at:])))
        at += len(names)
    k_buf, v_buf, op_buf, wg, wu, wd = (m[k] for k in ("k_buf", "v_buf", "op_buf", "wg", "wu", "wd"))
    q_pad, kn, vn, scores, attn_out = (m[k] for k in ("q_pad", "kn", "vn", "scores", "attn_out"))
    info, res_send, res_recv, hidden, result = (m[k] for k in ("info", "res_send", "res_recv", "hidden", "result"))
    hidden_in = m["hidden_in"]
    info_pad, send_sems, recv_sems, local_sems = (m[k] for k in ("info_pad", "send_sems", "recv_sems", "local_sems"))

    attn = lax.axis_index("attn")
    me = {"y": attn // 2, "c": lax.rem(attn, 2), "z": lax.axis_index("tp"), "x": lax.axis_index("exp")}
    c, other = me["c"], 1 - me["c"]
    place = [tuple(me[a] for a in axes) for axes in STREAMS]

    def device(c=None, **steps):
        at = dict(me)
        for axis, step in steps.items():
            at[axis] = wrap(at[axis] + step)
        if c is not None:
            at["c"] = c
        return (at["y"] * 2 + at["c"], at["z"], at["x"])

    sibling = device(c=other)

    def local(src, dst, i):
        return pltpu.make_async_copy(src, dst, local_sems.at[i])

    op_copies = {
        j: local(out_proj.at[:, pl.ds(pl.multiple_of(wrap(me["z"] + j) * QD, QD), QD)], op_buf.at[j], j)
        for j in (2, 1, 3, 0)
    }
    w_copies = [local(w_gate.at[0], wg, 4), local(w_up.at[0], wu, 5)]
    k_copies, v_copies = [], []
    for i in range(R // CHUNK):
        some = pl.ds(i * CHUNK, CHUNK)
        k_copies.append(local(cache.at[some, 0], k_buf.at[some], 7 + 2 * i))
        v_copies.append(local(cache.at[some, 1], v_buf.at[some], 8 + 2 * i))

    def down_columns(z, s, h):
        return w_down.at[0, :, pl.ds(pl.multiple_of(z * QD + s * 512 + h * W, W), W)]

    def down_rows(core):
        return pl.ds(pl.multiple_of(core * W, W), W)

    for cp in k_copies + v_copies:
        cp.start()
    for j in (2, 1, 3, 0):
        op_copies[j].start()

    barrier = pltpu.get_barrier_semaphore()
    partners = [device(c=k, z=j) for j in (1, 2, 3) for k in (0, 1)] + [sibling]
    partners += [device(c=k, **{a: j}) for a in ("x", "y") for j in (1, 2, 3) for k in (0, 1)]
    for p in partners:
        pl.semaphore_signal(barrier, inc=1, device_id=p, device_id_type=MESH)

    table, classes = {}, {}

    def sem(key):
        if key not in table:
            table[key] = len(table)
            assert len(table) <= SEMS
        return recv_sems.at[table[key]]

    def left(kind):
        if kind not in classes:
            classes[kind] = len(classes)
            assert len(classes) <= SENDS
        return send_sems.at[classes[kind]]

    def send(src, dst, kind, key, to):
        pltpu.make_async_remote_copy(
            src_ref=src, dst_ref=dst, send_sem=left(kind), recv_sem=sem(key), device_id=to, device_id_type=MESH
        ).start()

    def arrived(dst, key):
        pltpu.make_async_remote_copy(
            src_ref=dst, dst_ref=dst, send_sem=send_sems.at[0], recv_sem=sem(key),
            device_id=sibling, device_id_type=MESH,
        ).wait_recv()

    def drain(src, kind):
        pltpu.make_async_remote_copy(
            src_ref=src, dst_ref=src, send_sem=left(kind), recv_sem=recv_sems.at[0],
            device_id=sibling, device_id_type=MESH,
        ).wait_send()

    info_pad[...] = jnp.zeros_like(info_pad)
    for s in range(4):
        hit = jnp.where(ids[...] == slot_expert[s], gate_w[...], 0.0)
        info_pad[s : s + 1, :R] = jnp.sum(hit, axis=0, keepdims=True)
    info[c, me["y"], me["x"]] = info_pad[...].T[:R]

    def res_part(h):
        return jnp.concatenate(
            [residual[:, pl.ds(pl.multiple_of(me["z"] * QD + s * 512 + h * W, W), W)] for s in range(3)], axis=1
        ).astype(F32)

    res_send[...] = res_part(other)
    hidden[c] = res_part(c)
    for h in range(8):
        if h < HEADS:
            q_pad[pl.ds(h, R, stride=8), :] = query[:, h * HD : (h + 1) * HD].astype(F32)
        else:
            q_pad[pl.ds(h, R, stride=8), :] = jnp.zeros((R, HD), F32)
        kn[pl.ds(h, R, stride=8), :] = new_kv[:, 0, :].astype(F32)
        vn[pl.ds(h, R, stride=8), :] = new_kv[:, 1, :].astype(F32)

    def begin_links():
        pl.semaphore_wait(barrier, len(partners))
        send(res_send, res_recv, "res", "res", sibling)

    def info_1():
        for j in (1, 3, 2):
            spot = info.at[c, me["y"], me["x"]]
            send(spot, spot, "ix", "ix", device(x=j))

    def info_2():
        arrived(info.at[c, 0, pl.ds(0, 3)], "ix")
        for j in (1, 3, 2):
            spot = info.at[c, me["y"]]
            send(spot, spot, "iy", "iy", device(y=j))

    def info_3():
        arrived(info.at[c, pl.ds(0, 3)], "iy")
        send(info.at[c], info.at[c], "ic", "ic", sibling)

    def load_weights():
        for cp in w_copies:
            cp.start()
        for z in range(4):
            for s in range(3):
                send(down_columns(z, s, other), wd.at[z, s, down_rows(c)], "wd", "wd", sibling)
                local(down_columns(z, s, c), wd.at[z, s, down_rows(c)], 6).start()

    def pack(v):
        return jnp.concatenate([v[:, :384], v[:, 384:]], axis=0).astype(BF16)

    def flow(t):
        r0, n = PARTS[t]
        b = 2 * n
        p = buffers[t]
        z_send, z_recv, z_sib, z_own = (p[k] for k in ("z_send", "z_recv", "z_sib", "z_own"))
        x_all, ssum, acc_g, acc_u, act = (p[k] for k in ("x_all", "ssum", "acc_g", "acc_u", "act"))
        part, d2_in, plane_in = (p[k] for k in ("part", "d2_in", "plane_in"))
        row_out, row_in, row_own, blk_out, blk_in = (p[k] for k in ("row_out", "row_in", "row_own", "blk_out", "blk_in"))
        fin_send, fin = p["fin_send"], p["fin"]

        scale = HD ** (-0.5)
        position = lax.broadcasted_iota(jnp.int32, (8, CACHE), 1)
        mine8 = slice(r0 * 8, (r0 + n) * 8)
        for r in range(r0, r0 + n):
            if r % CHUNK == 0:
                k_copies[r // CHUNK].wait()
            s = lax.dot_general(
                q_pad[r * 8 : r * 8 + 8, :].astype(BF16), k_buf[r], (((1,), (1,)), ((), ())),
                preferred_element_type=F32,
            ) * scale
            scores[r * 8 : r * 8 + 8, :] = jnp.where(position < lengths[r], s, -1e30)
        own_score = jnp.sum(q_pad[mine8, :] * kn[mine8, :], axis=1, keepdims=True) * scale
        raw = scores[mine8, :]
        top = jnp.maximum(jnp.max(raw, axis=1, keepdims=True), own_score)
        weight = jnp.exp(raw - top)
        own_weight = jnp.exp(own_score - top)
        total = jnp.sum(weight, axis=1, keepdims=True) + own_weight
        scores[mine8, :] = weight / total
        own_prob = (own_weight / total).astype(BF16).astype(F32)
        for r in range(r0, r0 + n):
            if r % CHUNK == 0:
                v_copies[r // CHUNK].wait()
            attn_out[r * 8 : r * 8 + 8, :] = jnp.dot(
                scores[r * 8 : r * 8 + 8, :].astype(BF16), v_buf[r], preferred_element_type=F32
            )
        attn_out[mine8, :] = attn_out[mine8, :] + own_prob * vn[mine8, :]
        attended = jnp.concatenate(
            [attn_out[pl.ds(r0 * 8 + h, n, stride=8), :] for h in range(HEADS)], axis=1
        ).astype(BF16)

        def unpack(v):
            v = v.astype(F32)
            return jnp.concatenate([v[:n], v[n:]], axis=1)

        for j in (2, 1, 3, 0):
            if t == 0:
                op_copies[j].wait()
            term = jnp.dot(attended, op_buf[j], preferred_element_type=F32)
            halves = [
                jnp.concatenate([term[:, s * 512 + h * W : s * 512 + (h + 1) * W] for s in range(3)], axis=1)
                for h in range(2)
            ]
            if j == 2 and t == 0:
                begin_links()
            if j:
                for h in range(2):
                    z_send[j - 1, h] = pack(halves[h])
                    send(z_send.at[j - 1, h], z_recv.at[j - 1, c], ("z", t), ("z", t), device(c=h, z=j))
            else:
                z_own[0] = halves[0]
                z_own[1] = halves[1]
                z_sib[0] = pack(z_own[other])
                send(z_sib.at[0], z_sib.at[1], ("zs", t), ("zs", t), sibling)
        info_1()
        load_weights()
        acc_g[...] = jnp.zeros_like(acc_g)
        acc_u[...] = jnp.zeros_like(acc_u)
        ssum[...] = jnp.zeros_like(ssum)

        def pass_on(s, j):
            p1, p2, p3 = place[s]
            spot = x_all.at[c, s, p3, p2, wrap(p1 - j)]
            for k in (1, 3, 2):
                send(spot, spot, ("g2", t), ("g2", t, k), device(**{STREAMS[s][1]: k}))
            for k in (1, 3):
                send(spot, spot, ("g3", t), ("g3", t, 0), device(**{STREAMS[s][2]: k}))

        if t == 0:
            arrived(res_recv, "res")
            hidden[other] = res_recv[...]
        arrived(z_sib.at[1], ("zs", t))
        rows = slice(r0, r0 + n)
        mine = hidden[c, rows] + z_own[c]
        theirs = hidden[other, rows] + unpack(z_sib[1])
        arrived(z_recv, ("z", t))
        for j in range(3):
            mine = mine + unpack(z_recv[j, c])
            theirs = theirs + unpack(z_recv[j, other])
        hidden[c, rows] = mine
        hidden[other, rows] = theirs
        sent = jnp.concatenate([hidden[0, rows], hidden[1, rows]], axis=0).astype(BF16)
        for s, (a1, a2, a3) in enumerate(STREAMS):
            p1, p2, p3 = place[s]
            x_all[c, s, p3, p2, p1] = sent[:, s * W : (s + 1) * W]
            for j in (1, 3, 2):
                spot = x_all.at[c, s, p3, p2, p1]
                send(spot, spot, ("g1", t), ("g1", t, j), device(**{a1: j}))
        for s in range(3):
            pass_on(s, 0)
        send(hidden.at[other], hidden_in, "hid", "hid", sibling)

        def row(s, j3, j2, core):
            _, p2, p3 = place[s]
            return x_all.at[core, s, wrap(p3 + j3), wrap(p2 + j2)]

        def share_key(j3, j2):
            if j3 == 0:
                return ("gs", t, 0, j2 == 0)
            if j3 == 2:
                return ("gs", t, 2, j2 == 2)
            return ("gs", t, 1, j2 in (0, 1))

        def share(s, j3, j2):
            spot = row(s, j3, j2, c)
            send(spot, spot, ("gs", t), share_key(j3, j2), sibling)

        def shared(j3, j2):
            key = share_key(j3, j2)
            if j3 == 1:
                arrived(x_all.at[other, :, 0], key)
            elif key[3]:
                arrived(x_all.at[other, :, 0, 0], key)
            else:
                arrived(x_all.at[other, :, 0, pl.ds(0, 3)], key)

        def take1():
            for j in (1, 3, 2):
                arrived(x_all.at[c, :, 0, 0, 0], ("g1", t, j))
                for s in range(3):
                    pass_on(s, j)
            for s in range(3):
                share(s, 0, 0)

        def take2(j):
            arrived(x_all.at[c, :, 0, 0], ("g2", t, j))
            for s in range(3):
                spot = row(s, 0, 4 - j, c)
                for k in (1, 3):
                    send(spot, spot, ("g3", t), ("g3", t, 4 - j), device(**{STREAMS[s][2]: k}))
                share(s, 0, 4 - j)

        def take3(j2):
            arrived(x_all.at[c, :, 0, pl.ds(0, 2)], ("g3", t, j2))
            for s in range(3):
                for j in (1, 3):
                    spot = row(s, -j, j2, c)
                    half = spot.at[pl.ds(0 if j == 1 else 2, 2)]
                    send(half, half, ("g3", t), ("g4", t, j2), device(**{STREAMS[s][2]: j}))
                    share(s, 4 - j, j2)

        def take4(j2):
            arrived(x_all.at[c, :, 0, 0], ("g4", t, j2))
            for s in range(3):
                share(s, 2, j2)

        def multiply(xs, k0, spots):
            g = u = sq = None
            for h in range(2):
                x = jnp.concatenate([v.reshape(4 * b, W) for v in xs[h]], axis=0).astype(F32)
                k = k0 + h
                part_sq = x * x
                part_sq = part_sq[:, :128] + part_sq[:, 128:]
                xb = (x * gain[k]).astype(BF16)
                weight_rows = pl.ds(pl.multiple_of(k * W, W), W)
                part_g = jnp.dot(xb, wg[weight_rows, :], preferred_element_type=F32)
                part_u = jnp.dot(xb, wu[weight_rows, :], preferred_element_type=F32)
                g = part_g if g is None else g + part_g
                u = part_u if u is None else u + part_u
                sq = part_sq if sq is None else sq + part_sq
            for i, spot in enumerate(spots):
                m4 = slice(i * 4 * b, (i + 1) * 4 * b)
                acc_g[spot] = acc_g[spot] + g[m4].reshape(4, b, W)
                acc_u[spot] = acc_u[spot] + u[m4].reshape(4, b, W)
                ssum[spot] = ssum[spot] + sq[m4].reshape(4, b, 128)

        def rows_01(j3s, j2s):
            qs = [[wrap(place[s][2] + j3) for j3 in j3s] for s in range(2)]
            rs = [[wrap(place[s][1] + j2) for j2 in j2s] for s in range(2)]
            for q in qs[0]:
                multiply([[x_all[h, 0, q, r] for r in rs[0]] for h in range(2)], q * 6, [(r,) for r in rs[0]])
            for r in rs[1]:
                xs = [[x_all[h, 1, q, r] for q in qs[1]] for h in range(2)]
                multiply(xs, r * 6 + 2, [(slice(None), q) for q in qs[1]])

        def planes_2(j3s):
            qs = [wrap(place[2][2] + j3) for j3 in j3s]
            for z in range(4):
                multiply([[x_all[h, 2, q, :, z] for q in qs] for h in range(2)], z * 6 + 4, [(q,) for q in qs])

        take1()
        if t == 0:
            for cp in w_copies:
                cp.wait()
        take2(1)
        take2(3)
        take2(2)
        take3(0)
        info_2()
        shared(0, 0)
        shared(0, 1)
        rows_01((0,), (0, 1, 3, 2))
        take3(1)
        planes_2((0,))
        take3(3)
        shared(1, 0)
        rows_01((1, 3), (0, 1))
        take3(2)
        take4(0)
        take4(1)
        info_3()
        shared(1, 3)
        rows_01((1, 3), (3, 2))
        take4(3)
        planes_2((1, 3))
        take4(2)
        shared(2, 0)
        rows_01((2,), (0, 1, 3))
        shared(2, 2)
        rows_01((2,), (2,))
        planes_2((2,))

        if t == 0:
            arrived(info.at[other], "ic")
        lane4 = lax.broadcasted_iota(jnp.int32, (4, b, 128), 2)

        def activate(step, carry):
            i = wrap(me["y"] + 2 + step)
            both = jnp.concatenate([info[0, i, :, rows], info[1, i, :, rows]], axis=1)
            chosen = jnp.sum(jnp.where(lane4 == me["x"], both, 0.0), axis=2, keepdims=True)
            inv = lax.rsqrt(jnp.sum(ssum[i], axis=2, keepdims=True) / D + 1e-05)
            g = acc_g[i] * inv
            u = acc_u[i] * inv
            act[c, i] = (g / (1.0 + jnp.exp(-g)) * u * chosen).astype(BF16)
            send(act.at[c, i], act.at[c, i], ("act", t), key, sibling)
            return carry

        key = ("act", t, 0)
        activate(0, 0)
        key = ("act", t, 1)
        for step in (1, 2, 3):
            activate(step, 0)
        if t == 0:
            local(wd.at[:, :, down_rows(0)], wd.at[:, :, down_rows(0)], 6).wait()
            arrived(wd.at[:, :, down_rows(0)], "wd")
        arrived(act.at[other, 0], ("act", t, 0))

        def down(s, j3):
            q = wrap(place[s][2] + j3)

            def step(i, carry):
                pick = (i,) if s == 0 else ((slice(None), q) if s == 1 else (q,))
                a = jnp.concatenate([act[(h,) + pick].reshape(4 * b, W) for h in range(2)], axis=1)
                w = wd[q if s == 0 else i, s]
                y = jnp.dot(a, w, preferred_element_type=F32).reshape(4, b, W).astype(BF16)
                if s == 2:
                    part[s, j3, :, i] = y
                else:
                    part[s, j3, i] = y
                return carry

            lax.fori_loop(0, 4, step, 0, unroll=4)

        def second(s, j2):
            return wrap(place[s][1] + j2)

        def send_far(s):
            for j2 in (2, 3, 1, 0):
                j = 1 if j2 in FORWARD_UP else 3
                r = second(s, j2)
                send(part.at[s, 2, r], d2_in.at[s, r], ("r4", t), ("r4", t, j2), device(**{STREAMS[s][2]: j}))

        def send_near(s, j, j2):
            r = second(s, j2)
            to = device(**{STREAMS[s][2]: j})
            send(part.at[s, j, r], plane_in.at[s, j // 2, r], ("r3", t), ("r3", t, j2), to)

        def add_far(j2):
            j = 1 if j2 in FORWARD_UP else 3
            arrived(d2_in.at[:, 0], ("r4", t, j2))
            for s in range(3):
                r = second(s, j2)
                part[s, j, r] = (part[s, j, r].astype(F32) + d2_in[s, r].astype(F32)).astype(BF16)
                send_near(s, j, j2)

        down(2, 2)
        send_far(2)
        arrived(act.at[other, pl.ds(0, 3)], ("act", t, 1))
        for s in range(2):
            down(s, 2)
            send_far(s)
        for s in range(3):
            down(s, 1)
            send_near(s, 1, 2)
            down(s, 3)
            send_near(s, 3, 3)
        for s in range(3):
            down(s, 0)
        add_far(2)
        add_far(3)
        for s in range(3):
            send_near(s, 1, 1)
        add_far(1)
        add_far(0)
        for s in range(3):
            send_near(s, 3, 0)
        for j2 in (2, 3, 1, 0):
            arrived(plane_in.at[:, :, 0], ("r3", t, j2))
            for s in range(3):
                r = second(s, j2)
                v = part[s, 0, r].astype(F32) + plane_in[s, 0, r].astype(F32) + plane_in[s, 1, r].astype(F32)
                if j2:
                    row_out[s, j2 - 1] = v.astype(BF16)
                    to = device(**{STREAMS[s][1]: j2})
                    send(row_out.at[s, j2 - 1], row_in.at[s, j2 - 1], ("r2", t), ("r2", t, s), to)
                else:
                    row_own[s] = v
        def fold(v):
            return jnp.concatenate([v[:, :128], v[:, 128:]], axis=0).astype(BF16)

        def unfold(v):
            v = v.astype(F32)
            return jnp.concatenate([v[:n], v[n:]], axis=1)

        for s in range(3):
            arrived(row_in.at[s], ("r2", t, s))
            row_own[s] = row_own[s] + (
                row_in[s, 0].astype(F32) + row_in[s, 1].astype(F32) + row_in[s, 2].astype(F32)
            )
            for j1 in (2, 1, 3):
                v = row_own[s, wrap(place[s][0] + j1)]
                for k in range(2):
                    blk_out[s, j1 - 1, k] = fold(v[k * n : (k + 1) * n])
                    to = device(c=k, **{STREAMS[s][0]: j1})
                    send(blk_out.at[s, j1 - 1, k], blk_in.at[s, j1 - 1, c], ("r1", t), ("r1", t, s), to)
            v = row_own[s, place[s][0]]
            for k in range(2):
                fin_send[k, s] = v[k * n : (k + 1) * n]
            send(fin_send.at[other, s], fin.at[s], ("fin", t), ("fin", t), sibling)
        drain(z_send, ("z", t))
        drain(z_sib.at[0], ("zs", t))
        drain(x_all.at[c, :, 0, 0, pl.ds(0, 3)], ("g1", t))
        drain(x_all.at[c, :, 0, pl.ds(0, 3)], ("g2", t))
        drain(x_all.at[c, :, pl.ds(0, 3)], ("g3", t))
        drain(x_all.at[c], ("gs", t))
        drain(act.at[c], ("act", t))
        drain(d2_in, ("r4", t))
        drain(plane_in, ("r3", t))
        drain(row_out, ("r2", t))
        drain(hidden_in, "hid")
        arrived(hidden_in, "hid")
        arrived(fin, ("fin", t))
        drain(fin, ("fin", t))
        for s in range(3):
            cols = slice(s * W, (s + 1) * W)
            mine = hidden[c, :, cols] + fin_send[c, s]
            theirs = hidden_in[:, cols] + fin[s]
            arrived(blk_in.at[s], ("r1", t, s))
            for j in range(3):
                mine = mine + unfold(blk_in[s, j, c])
                theirs = theirs + unfold(blk_in[s, j, other])
            fin_send[c, s] = mine
            fin_send[other, s] = theirs
            for h in range(2):
                result[rows, s * 512 + h * W : s * 512 + (h + 1) * W] = fin_send[h, s]
        drain(blk_out, ("r1", t))

    flow(0)
    drain(res_send, "res")
    drain(info.at[c, 0, pl.ds(0, 3)], "ix")
    drain(info.at[c, pl.ds(0, 3)], "iy")
    drain(info.at[c], "ic")
    drain(wd.at[:, :, down_rows(0)], "wd")
    out[...] = result[...].astype(BF16)


def local_step(
    new_query, new_kv, kv_cache, lengths, residual, out_proj, expert_ids, gate_weights, slot_expert, moe_gain,
    w_gate, w_up, w_down,
):
    vmem = pl.BlockSpec(memory_space=pltpu.VMEM)
    smem = pl.BlockSpec(memory_space=pltpu.SMEM)
    anywhere = pl.BlockSpec(memory_space=pl.ANY)
    scratch = list(common_scratch().values())
    for _, n in PARTS:
        scratch += list(part_scratch(n).values())
    return pl.pallas_call(
        kernel,
        out_shape=jax.ShapeDtypeStruct((R, QD), BF16),
        in_specs=[smem, smem] + [vmem] * 6 + [anywhere] * 5,
        out_specs=vmem,
        scratch_shapes=scratch,
        compiler_params=pltpu.CompilerParams(
            collective_id=0, has_side_effects=True, vmem_limit_bytes=62 * 2**20
        ),
        name="decode_layer",
    )(
        lengths, slot_expert, new_query, new_kv, residual, expert_ids.T, gate_weights.T,
        moe_gain.reshape(D // W, 1, W), kv_cache, out_proj, w_gate, w_up, w_down,
    )


def solution(mesh):
    placed = (
        P(("attn", "exp"), "tp"),
        P(("attn", "exp"), None, "tp"),
        P(("attn", "exp"), None, None, "tp"),
        P(("attn", "exp")),
        P(("attn", "exp"), None),
        P("tp", None),
        P(("attn", "exp"), None),
        P(("attn", "exp"), None),
        P(),
        P(),
        P("exp", None, ("attn", "tp")),
        P("exp", None, ("attn", "tp")),
        P("exp", ("attn", "tp"), None),
    )
    return jax.shard_map(
        local_step, mesh=mesh, in_specs=placed, out_specs=P(("attn", "exp"), "tp"), check_vma=False
    )
```

```python
import jax
import jax.numpy as jnp
from jax import lax
from jax.experimental import pallas as pl
from jax.experimental.pallas import tpu as pltpu
from jax.sharding import PartitionSpec as P

MESH = pl.DeviceIdType.MESH
F32 = jnp.float32
BF16 = jnp.bfloat16

HD = 128
HEADS = 6
R = 24
CACHE = 512
D = 6144
QD = 1536
W = 256
SEMS = 46
SENDS = 20
PARTS = ((0, R),)
CHUNK = 6

STREAMS = (("x", "y", "z"), ("y", "z", "x"), ("z", "x", "y"))
FORWARD_UP = (0, 3)
FORWARD_DOWN = (1, 2)


def wrap(v):
    return lax.rem(v + 4, 4)


def common_scratch():
    v = pltpu.VMEM
    return dict(
        k_buf=v((R, CACHE, HD), BF16),
        v_buf=v((R, CACHE, HD), BF16),
        op_buf=v((4, HEADS * HD, QD), BF16),
        wg=v((D, W), BF16),
        wu=v((D, W), BF16),
        wd=v((4, 3, 2 * W, W), BF16),
        q_pad=v((R * 8, HD), F32),
        kn=v((R * 8, HD), F32),
        vn=v((R * 8, HD), F32),
        scores=v((R * 8, CACHE), F32),
        attn_out=v((R * 8, HD), F32),
        info_pad=v((128, 128), F32),
        info=v((2, 4, 4, R, 128), F32),
        res_send=v((R, 3 * W), F32),
        res_recv=v((R, 3 * W), F32),
        hidden=v((2, R, 3 * W), F32),
        hidden_in=v((R, 3 * W), F32),
        result=v((R, QD), F32),
        send_sems=pltpu.SemaphoreType.DMA((SENDS,)),
        recv_sems=pltpu.SemaphoreType.DMA((SEMS,)),
        local_sems=pltpu.SemaphoreType.DMA((7 + 2 * (R // CHUNK),)),
    )


def part_scratch(n):
    v, b = pltpu.VMEM, 2 * n
    return dict(
        z_send=v((3, 2, b, 384), BF16),
        z_recv=v((3, 2, b, 384), BF16),
        z_sib=v((2, b, 384), BF16),
        z_own=v((2, n, 3 * W), F32),
        x_all=v((2, 3, 4, 4, 4, b, W), BF16),
        ssum=v((4, 4, b, 128), F32),
        acc_g=v((4, 4, b, W), F32),
        acc_u=v((4, 4, b, W), F32),
        act=v((2, 4, 4, b, W), BF16),
        part=v((3, 4, 4, 4, b, W), BF16),
        d2_in=v((3, 4, 4, b, W), BF16),
        plane_in=v((3, 2, 4, 4, b, W), BF16),
        row_out=v((3, 3, 4, b, W), BF16),
        row_in=v((3, 3, 4, b, W), BF16),
        row_own=v((3, 4, b, W), F32),
        blk_out=v((3, 3, 2, b, 128), BF16),
        blk_in=v((3, 3, 2, b, 128), BF16),
        fin_send=v((2, 3, n, W), F32),
        fin=v((3, n, W), F32),
    )


def kernel(*refs):
    (lengths, slot_expert, query, new_kv, residual, ids, gate_w, gain, cache, out_proj, w_gate, w_up, w_down, out) = refs[:14]
    names = common_scratch()
    m = dict(zip(names, refs[14:]))
    at = 14 + len(names)
    buffers = []
    for _, n in PARTS:
        names = part_scratch(n)
        buffers.append(dict(zip(names, refs[at:])))
        at += len(names)
    k_buf, v_buf, op_buf, wg, wu, wd = (m[k] for k in ("k_buf", "v_buf", "op_buf", "wg", "wu", "wd"))
    q_pad, kn, vn, scores, attn_out = (m[k] for k in ("q_pad", "kn", "vn", "scores", "attn_out"))
    info, res_send, res_recv, hidden, result = (m[k] for k in ("info", "res_send", "res_recv", "hidden", "result"))
    hidden_in = m["hidden_in"]
    info_pad, send_sems, recv_sems, local_sems = (m[k] for k in ("info_pad", "send_sems", "recv_sems", "local_sems"))

    attn = lax.axis_index("attn")
    me = {"y": attn // 2, "c": lax.rem(attn, 2), "z": lax.axis_index("tp"), "x": lax.axis_index("exp")}
    c, other = me["c"], 1 - me["c"]
    place = [tuple(me[a] for a in axes) for axes in STREAMS]

    def device(c=None, **steps):
        at = dict(me)
        for axis, step in steps.items():
            at[axis] = wrap(at[axis] + step)
        if c is not None:
            at["c"] = c
        return (at["y"] * 2 + at["c"], at["z"], at["x"])

    sibling = device(c=other)

    def local(src, dst, i):
        return pltpu.make_async_copy(src, dst, local_sems.at[i])

    op_copies = {
        j: local(out_proj.at[:, pl.ds(pl.multiple_of(wrap(me["z"] + j) * QD, QD), QD)], op_buf.at[j], j)
        for j in (2, 1, 3, 0)
    }
    w_copies = [local(w_gate.at[0], wg, 4), local(w_up.at[0], wu, 5)]
    k_copies, v_copies = [], []
    for i in range(R // CHUNK):
        some = pl.ds(i * CHUNK, CHUNK)
        k_copies.append(local(cache.at[some, 0], k_buf.at[some], 7 + 2 * i))
        v_copies.append(local(cache.at[some, 1], v_buf.at[some], 8 + 2 * i))

    def down_columns(z, s, h):
        return w_down.at[0, :, pl.ds(pl.multiple_of(z * QD + s * 512 + h * W, W), W)]

    def down_rows(core):
        return pl.ds(pl.multiple_of(core * W, W), W)

    for cp in k_copies + v_copies:
        cp.start()
    for j in (2, 1, 3, 0):
        op_copies[j].start()

    barrier = pltpu.get_barrier_semaphore()
    partners = [device(c=k, z=j) for j in (1, 2, 3) for k in (0, 1)] + [sibling]
    partners += [device(c=k, **{a: j}) for a in ("x", "y") for j in (1, 2, 3) for k in (0, 1)]
    for p in partners:
        pl.semaphore_signal(barrier, inc=1, device_id=p, device_id_type=MESH)

    table, classes = {}, {}

    def sem(key):
        if key not in table:
            table[key] = len(table)
            assert len(table) <= SEMS
        return recv_sems.at[table[key]]

    def left(kind):
        if kind not in classes:
            classes[kind] = len(classes)
            assert len(classes) <= SENDS
        return send_sems.at[classes[kind]]

    def send(src, dst, kind, key, to):
        pltpu.make_async_remote_copy(
            src_ref=src, dst_ref=dst, send_sem=left(kind), recv_sem=sem(key), device_id=to, device_id_type=MESH
        ).start()

    def arrived(dst, key):
        pltpu.make_async_remote_copy(
            src_ref=dst, dst_ref=dst, send_sem=send_sems.at[0], recv_sem=sem(key),
            device_id=sibling, device_id_type=MESH,
        ).wait_recv()

    def drain(src, kind):
        pltpu.make_async_remote_copy(
            src_ref=src, dst_ref=src, send_sem=left(kind), recv_sem=recv_sems.at[0],
            device_id=sibling, device_id_type=MESH,
        ).wait_send()

    info_pad[...] = jnp.zeros_like(info_pad)
    for s in range(4):
        hit = jnp.where(ids[...] == slot_expert[s], gate_w[...], 0.0)
        info_pad[s : s + 1, :R] = jnp.sum(hit, axis=0, keepdims=True)
    info[c, me["y"], me["x"]] = info_pad[...].T[:R]

    def res_part(h):
        return jnp.concatenate(
            [residual[:, pl.ds(pl.multiple_of(me["z"] * QD + s * 512 + h * W, W), W)] for s in range(3)], axis=1
        ).astype(F32)

    res_send[...] = res_part(other)
    hidden[c] = res_part(c)
    for h in range(8):
        if h < HEADS:
            q_pad[pl.ds(h, R, stride=8), :] = query[:, h * HD : (h + 1) * HD].astype(F32)
        else:
            q_pad[pl.ds(h, R, stride=8), :] = jnp.zeros((R, HD), F32)
        kn[pl.ds(h, R, stride=8), :] = new_kv[:, 0, :].astype(F32)
        vn[pl.ds(h, R, stride=8), :] = new_kv[:, 1, :].astype(F32)

    def begin_links():
        pl.semaphore_wait(barrier, len(partners))
        send(res_send, res_recv, "res", "res", sibling)

    def info_1():
        for j in (1, 3, 2):
            spot = info.at[c, me["y"], me["x"]]
            send(spot, spot, "ix", "ix", device(x=j))

    def info_2():
        arrived(info.at[c, 0, pl.ds(0, 3)], "ix")
        for j in (1, 3, 2):
            spot = info.at[c, me["y"]]
            send(spot, spot, "iy", "iy", device(y=j))

    def info_3():
        arrived(info.at[c, pl.ds(0, 3)], "iy")
        send(info.at[c], info.at[c], "ic", "ic", sibling)

    def load_weights():
        for cp in w_copies:
            cp.start()
        for z in range(4):
            for s in range(3):
                send(down_columns(z, s, other), wd.at[z, s, down_rows(c)], "wd", "wd", sibling)
                local(down_columns(z, s, c), wd.at[z, s, down_rows(c)], 6).start()

    def pack(v):
        return jnp.concatenate([v[:, :384], v[:, 384:]], axis=0).astype(BF16)

    def flow(t):
        r0, n = PARTS[t]
        b = 2 * n
        p = buffers[t]
        z_send, z_recv, z_sib, z_own = (p[k] for k in ("z_send", "z_recv", "z_sib", "z_own"))
        x_all, ssum, acc_g, acc_u, act = (p[k] for k in ("x_all", "ssum", "acc_g", "acc_u", "act"))
        part, d2_in, plane_in = (p[k] for k in ("part", "d2_in", "plane_in"))
        row_out, row_in, row_own, blk_out, blk_in = (p[k] for k in ("row_out", "row_in", "row_own", "blk_out", "blk_in"))
        fin_send, fin = p["fin_send"], p["fin"]

        scale = HD ** (-0.5)
        position = lax.broadcasted_iota(jnp.int32, (8, CACHE), 1)
        mine8 = slice(r0 * 8, (r0 + n) * 8)
        for r in range(r0, r0 + n):
            if r % CHUNK == 0:
                k_copies[r // CHUNK].wait()
            s = lax.dot_general(
                q_pad[r * 8 : r * 8 + 8, :].astype(BF16), k_buf[r], (((1,), (1,)), ((), ())),
                preferred_element_type=F32,
            ) * scale
            scores[r * 8 : r * 8 + 8, :] = jnp.where(position < lengths[r], s, -1e30)
        own_score = jnp.sum(q_pad[mine8, :] * kn[mine8, :], axis=1, keepdims=True) * scale
        raw = scores[mine8, :]
        top = jnp.maximum(jnp.max(raw, axis=1, keepdims=True), own_score)
        weight = jnp.exp(raw - top)
        own_weight = jnp.exp(own_score - top)
        total = jnp.sum(weight, axis=1, keepdims=True) + own_weight
        scores[mine8, :] = weight / total
        own_prob = (own_weight / total).astype(BF16).astype(F32)
        for r in range(r0, r0 + n):
            if r % CHUNK == 0:
                v_copies[r // CHUNK].wait()
            attn_out[r * 8 : r * 8 + 8, :] = jnp.dot(
                scores[r * 8 : r * 8 + 8, :].astype(BF16), v_buf[r], preferred_element_type=F32
            )
        attn_out[mine8, :] = attn_out[mine8, :] + own_prob * vn[mine8, :]
        attended = jnp.concatenate(
            [attn_out[pl.ds(r0 * 8 + h, n, stride=8), :] for h in range(HEADS)], axis=1
        ).astype(BF16)

        def unpack(v):
            v = v.astype(F32)
            return jnp.concatenate([v[:n], v[n:]], axis=1)

        for j in (2, 1, 3, 0):
            if t == 0:
                op_copies[j].wait()
            term = jnp.dot(attended, op_buf[j], preferred_element_type=F32)
            halves = [
                jnp.concatenate([term[:, s * 512 + h * W : s * 512 + (h + 1) * W] for s in range(3)], axis=1)
                for h in range(2)
            ]
            if j == 2 and t == 0:
                begin_links()
            if j:
                for h in range(2):
                    z_send[j - 1, h] = pack(halves[h])
                    send(z_send.at[j - 1, h], z_recv.at[j - 1, c], ("z", t), ("z", t), device(c=h, z=j))
            else:
                z_own[0] = halves[0]
                z_own[1] = halves[1]
                z_sib[0] = pack(z_own[other])
                send(z_sib.at[0], z_sib.at[1], ("zs", t), ("zs", t), sibling)
        info_1()
        load_weights()
        acc_g[...] = jnp.zeros_like(acc_g)
        acc_u[...] = jnp.zeros_like(acc_u)
        ssum[...] = jnp.zeros_like(ssum)

        def pass_on(s, j):
            p1, p2, p3 = place[s]
            spot = x_all.at[c, s, p3, p2, wrap(p1 - j)]
            for k in (1, 3, 2):
                send(spot, spot, ("g2", t), ("g2", t, k), device(**{STREAMS[s][1]: k}))
            for k in (1, 3):
                send(spot, spot, ("g3", t), ("g3", t, 0), device(**{STREAMS[s][2]: k}))

        if t == 0:
            arrived(res_recv, "res")
            hidden[other] = res_recv[...]
        arrived(z_sib.at[1], ("zs", t))
        rows = slice(r0, r0 + n)
        mine = hidden[c, rows] + z_own[c]
        theirs = hidden[other, rows] + unpack(z_sib[1])
        arrived(z_recv, ("z", t))
        for j in range(3):
            mine = mine + unpack(z_recv[j, c])
            theirs = theirs + unpack(z_recv[j, other])
        hidden[c, rows] = mine
        hidden[other, rows] = theirs
        sent = jnp.concatenate([hidden[0, rows], hidden[1, rows]], axis=0).astype(BF16)
        for s, (a1, a2, a3) in enumerate(STREAMS):
            p1, p2, p3 = place[s]
            x_all[c, s, p3, p2, p1] = sent[:, s * W : (s + 1) * W]
            for j in (1, 3, 2):
                spot = x_all.at[c, s, p3, p2, p1]
                send(spot, spot, ("g1", t), ("g1", t, j), device(**{a1: j}))
        for s in range(3):
            pass_on(s, 0)
        send(hidden.at[other], hidden_in, "hid", "hid", sibling)

        def row(s, j3, j2, core):
            _, p2, p3 = place[s]
            return x_all.at[core, s, wrap(p3 + j3), wrap(p2 + j2)]

        def share_key(j3, j2):
            if j3 == 0:
                return ("gs", t, 0, j2 == 0)
            if j3 == 2:
                return ("gs", t, 2, j2 == 2)
            return ("gs", t, 1, j2 in (0, 1))

        def share(s, j3, j2):
            spot = row(s, j3, j2, c)
            send(spot, spot, ("gs", t), share_key(j3, j2), sibling)

        def shared(j3, j2):
            key = share_key(j3, j2)
            if j3 == 1:
                arrived(x_all.at[other, :, 0], key)
            elif key[3]:
                arrived(x_all.at[other, :, 0, 0], key)
            else:
                arrived(x_all.at[other, :, 0, pl.ds(0, 3)], key)

        def take1():
            for j in (1, 3, 2):
                arrived(x_all.at[c, :, 0, 0, 0], ("g1", t, j))
                for s in range(3):
                    pass_on(s, j)
            for s in range(3):
                share(s, 0, 0)

        def take2(j):
            arrived(x_all.at[c, :, 0, 0], ("g2", t, j))
            for s in range(3):
                spot = row(s, 0, 4 - j, c)
                for k in (1, 3):
                    send(spot, spot, ("g3", t), ("g3", t, 4 - j), device(**{STREAMS[s][2]: k}))
                share(s, 0, 4 - j)

        def take3(j2):
            arrived(x_all.at[c, :, 0, pl.ds(0, 2)], ("g3", t, j2))
            for s in range(3):
                for j in (1, 3):
                    spot = row(s, -j, j2, c)
                    half = spot.at[pl.ds(0 if j == 1 else 2, 2)]
                    send(half, half, ("g3", t), ("g4", t, j2), device(**{STREAMS[s][2]: j}))
                    share(s, 4 - j, j2)

        def take4(j2):
            arrived(x_all.at[c, :, 0, 0], ("g4", t, j2))
            for s in range(3):
                share(s, 2, j2)

        def multiply(xs, k0, spots):
            g = u = sq = None
            for h in range(2):
                x = jnp.concatenate([v.reshape(4 * b, W) for v in xs[h]], axis=0).astype(F32)
                k = k0 + h
                part_sq = x * x
                part_sq = part_sq[:, :128] + part_sq[:, 128:]
                xb = (x * gain[k]).astype(BF16)
                weight_rows = pl.ds(pl.multiple_of(k * W, W), W)
                part_g = jnp.dot(xb, wg[weight_rows, :], preferred_element_type=F32)
                part_u = jnp.dot(xb, wu[weight_rows, :], preferred_element_type=F32)
                g = part_g if g is None else g + part_g
                u = part_u if u is None else u + part_u
                sq = part_sq if sq is None else sq + part_sq
            for i, spot in enumerate(spots):
                m4 = slice(i * 4 * b, (i + 1) * 4 * b)
                acc_g[spot] = acc_g[spot] + g[m4].reshape(4, b, W)
                acc_u[spot] = acc_u[spot] + u[m4].reshape(4, b, W)
                ssum[spot] = ssum[spot] + sq[m4].reshape(4, b, 128)

        def rows_01(j3s, j2s):
            qs = [[wrap(place[s][2] + j3) for j3 in j3s] for s in range(2)]
            rs = [[wrap(place[s][1] + j2) for j2 in j2s] for s in range(2)]
            for q in qs[0]:
                multiply([[x_all[h, 0, q, r] for r in rs[0]] for h in range(2)], q * 6, [(r,) for r in rs[0]])
            for r in rs[1]:
                xs = [[x_all[h, 1, q, r] for q in qs[1]] for h in range(2)]
                multiply(xs, r * 6 + 2, [(slice(None), q) for q in qs[1]])

        def planes_2(j3s):
            qs = [wrap(place[2][2] + j3) for j3 in j3s]
            for z in range(4):
                multiply([[x_all[h, 2, q, :, z] for q in qs] for h in range(2)], z * 6 + 4, [(q,) for q in qs])

        take1()
        if t == 0:
            for cp in w_copies:
                cp.wait()
        take2(1)
        take2(3)
        take2(2)
        take3(0)
        info_2()
        shared(0, 0)
        shared(0, 1)
        rows_01((0,), (0, 1, 3, 2))
        take3(1)
        planes_2((0,))
        take3(3)
        shared(1, 0)
        rows_01((1, 3), (0, 1))
        take3(2)
        take4(0)
        take4(1)
        info_3()
        shared(1, 3)
        rows_01((1, 3), (3, 2))
        take4(3)
        planes_2((1, 3))
        take4(2)
        shared(2, 0)
        rows_01((2,), (0, 1, 3))
        shared(2, 2)
        rows_01((2,), (2,))
        planes_2((2,))

        if t == 0:
            arrived(info.at[other], "ic")
        lane4 = lax.broadcasted_iota(jnp.int32, (4, b, 128), 2)

        def activate(step, carry):
            i = wrap(me["y"] + 2 + step)
            both = jnp.concatenate([info[0, i, :, rows], info[1, i, :, rows]], axis=1)
            chosen = jnp.sum(jnp.where(lane4 == me["x"], both, 0.0), axis=2, keepdims=True)
            inv = lax.rsqrt(jnp.sum(ssum[i], axis=2, keepdims=True) / D + 1e-05)
            g = acc_g[i] * inv
            u = acc_u[i] * inv
            act[c, i] = (g / (1.0 + jnp.exp(-g)) * u * chosen).astype(BF16)
            send(act.at[c, i], act.at[c, i], ("act", t), key, sibling)
            return carry

        key = ("act", t, 0)
        activate(0, 0)
        key = ("act", t, 1)
        for step in (1, 2, 3):
            activate(step, 0)
        if t == 0:
            local(wd.at[:, :, down_rows(0)], wd.at[:, :, down_rows(0)], 6).wait()
            arrived(wd.at[:, :, down_rows(0)], "wd")
        arrived(act.at[other, 0], ("act", t, 0))

        def down(s, j3, steps=None):
            q = wrap(place[s][2] + j3)

            def step(i, carry):
                pick = (i,) if s == 0 else ((slice(None), q) if s == 1 else (q,))
                a = jnp.concatenate([act[(h,) + pick].reshape(4 * b, W) for h in range(2)], axis=1)
                w = wd[q if s == 0 else i, s]
                y = jnp.dot(a, w, preferred_element_type=F32).reshape(4, b, W).astype(BF16)
                if s == 2:
                    part[s, j3, :, i] = y
                else:
                    part[s, j3, i] = y
                return carry

            if steps is None:
                lax.fori_loop(0, 4, step, 0, unroll=4)
            else:
                for i in steps:
                    step(i, 0)

        def second(s, j2):
            return wrap(place[s][1] + j2)

        def send_far(s, rows=(2, 3, 1, 0)):
            for j2 in rows:
                j = 1 if j2 in FORWARD_UP else 3
                r = second(s, j2)
                send(part.at[s, 2, r], d2_in.at[s, r], ("r4", t), ("r4", t, j2), device(**{STREAMS[s][2]: j}))

        def send_near(s, j, j2):
            r = second(s, j2)
            to = device(**{STREAMS[s][2]: j})
            send(part.at[s, j, r], plane_in.at[s, j // 2, r], ("r3", t), ("r3", t, j2), to)

        def add_far(j2):
            j = 1 if j2 in FORWARD_UP else 3
            arrived(d2_in.at[:, 0], ("r4", t, j2))
            for s in range(3):
                r = second(s, j2)
                part[s, j, r] = (part[s, j, r].astype(F32) + d2_in[s, r].astype(F32)).astype(BF16)
                send_near(s, j, j2)

        down(2, 2)
        send_far(2)
        down(0, 2, [second(0, 2)])
        send_far(0, (2,))
        arrived(act.at[other, pl.ds(0, 3)], ("act", t, 1))
        down(0, 2, [second(0, j2) for j2 in (3, 1, 0)])
        send_far(0, (3, 1, 0))
        down(1, 2)
        send_far(1)
        for s in range(3):
            down(s, 1)
            send_near(s, 1, 2)
            down(s, 3)
            send_near(s, 3, 3)
        for s in range(3):
            down(s, 0)
        add_far(2)
        add_far(3)
        for s in range(3):
            send_near(s, 1, 1)
        add_far(1)
        add_far(0)
        for s in range(3):
            send_near(s, 3, 0)
        for j2 in (2, 3, 1, 0):
            arrived(plane_in.at[:, :, 0], ("r3", t, j2))
            for s in range(3):
                r = second(s, j2)
                v = part[s, 0, r].astype(F32) + plane_in[s, 0, r].astype(F32) + plane_in[s, 1, r].astype(F32)
                if j2:
                    row_out[s, j2 - 1] = v.astype(BF16)
                    to = device(**{STREAMS[s][1]: j2})
                    send(row_out.at[s, j2 - 1], row_in.at[s, j2 - 1], ("r2", t), ("r2", t, s), to)
                else:
                    row_own[s] = v
        def fold(v):
            return jnp.concatenate([v[:, :128], v[:, 128:]], axis=0).astype(BF16)

        def unfold(v):
            v = v.astype(F32)
            return jnp.concatenate([v[:n], v[n:]], axis=1)

        for s in range(3):
            arrived(row_in.at[s], ("r2", t, s))
            row_own[s] = row_own[s] + (
                row_in[s, 0].astype(F32) + row_in[s, 1].astype(F32) + row_in[s, 2].astype(F32)
            )
            for j1 in (2, 1, 3):
                v = row_own[s, wrap(place[s][0] + j1)]
                for k in range(2):
                    blk_out[s, j1 - 1, k] = fold(v[k * n : (k + 1) * n])
                    to = device(c=k, **{STREAMS[s][0]: j1})
                    send(blk_out.at[s, j1 - 1, k], blk_in.at[s, j1 - 1, c], ("r1", t), ("r1", t, s), to)
            v = row_own[s, place[s][0]]
            for k in range(2):
                fin_send[k, s] = v[k * n : (k + 1) * n]
            send(fin_send.at[other, s], fin.at[s], ("fin", t), ("fin", t), sibling)
        drain(z_send, ("z", t))
        drain(z_sib.at[0], ("zs", t))
        drain(x_all.at[c, :, 0, 0, pl.ds(0, 3)], ("g1", t))
        drain(x_all.at[c, :, 0, pl.ds(0, 3)], ("g2", t))
        drain(x_all.at[c, :, pl.ds(0, 3)], ("g3", t))
        drain(x_all.at[c], ("gs", t))
        drain(act.at[c], ("act", t))
        drain(d2_in, ("r4", t))
        drain(plane_in, ("r3", t))
        drain(row_out, ("r2", t))
        drain(hidden_in, "hid")
        arrived(hidden_in, "hid")
        arrived(fin, ("fin", t))
        drain(fin, ("fin", t))
        for s in range(3):
            cols = slice(s * W, (s + 1) * W)
            mine = hidden[c, :, cols] + fin_send[c, s]
            theirs = hidden_in[:, cols] + fin[s]
            arrived(blk_in.at[s], ("r1", t, s))
            for j in range(3):
                mine = mine + unfold(blk_in[s, j, c])
                theirs = theirs + unfold(blk_in[s, j, other])
            fin_send[c, s] = mine
            fin_send[other, s] = theirs
            for h in range(2):
                result[rows, s * 512 + h * W : s * 512 + (h + 1) * W] = fin_send[h, s]
        drain(blk_out, ("r1", t))

    flow(0)
    drain(res_send, "res")
    drain(info.at[c, 0, pl.ds(0, 3)], "ix")
    drain(info.at[c, pl.ds(0, 3)], "iy")
    drain(info.at[c], "ic")
    drain(wd.at[:, :, down_rows(0)], "wd")
    out[...] = result[...].astype(BF16)


def local_step(
    new_query, new_kv, kv_cache, lengths, residual, out_proj, expert_ids, gate_weights, slot_expert, moe_gain,
    w_gate, w_up, w_down,
):
    vmem = pl.BlockSpec(memory_space=pltpu.VMEM)
    smem = pl.BlockSpec(memory_space=pltpu.SMEM)
    anywhere = pl.BlockSpec(memory_space=pl.ANY)
    scratch = list(common_scratch().values())
    for _, n in PARTS:
        scratch += list(part_scratch(n).values())
    return pl.pallas_call(
        kernel,
        out_shape=jax.ShapeDtypeStruct((R, QD), BF16),
        in_specs=[smem, smem] + [vmem] * 6 + [anywhere] * 5,
        out_specs=vmem,
        scratch_shapes=scratch,
        compiler_params=pltpu.CompilerParams(
            collective_id=0, has_side_effects=True, vmem_limit_bytes=62 * 2**20
        ),
        name="decode_layer",
    )(
        lengths, slot_expert, new_query, new_kv, residual, expert_ids.T, gate_weights.T,
        moe_gain.reshape(D // W, 1, W), kv_cache, out_proj, w_gate, w_up, w_down,
    )


def solution(mesh):
    placed = (
        P(("attn", "exp"), "tp"),
        P(("attn", "exp"), None, "tp"),
        P(("attn", "exp"), None, None, "tp"),
        P(("attn", "exp")),
        P(("attn", "exp"), None),
        P("tp", None),
        P(("attn", "exp"), None),
        P(("attn", "exp"), None),
        P(),
        P(),
        P("exp", None, ("attn", "tp")),
        P("exp", None, ("attn", "tp")),
        P("exp", ("attn", "tp"), None),
    )
    return jax.shard_map(
        local_step, mesh=mesh, in_specs=placed, out_specs=P(("attn", "exp"), "tp"), check_vma=False
    )
```
